256 devices in a mesh: row: 4 (over y), col: 16 (over z, core), layer: 4 (over x).
Axes of the slice: x: 4, y: 4, z: 8, core: 2. Of those that a mesh axis runs over, the one named last changes fastest.
Arguments:
- matrix: bfloat16 [8192, 8192], P('row', 'col'), may hold values from -1.1953125 to 1.1953125
- pattern: int32 [256, 256], P('row', 'col'), may hold values from 0 to 1, as said below
- keep: int32 [256, 256], P('row', ('col', 'layer')), may hold values 0 or 1
Outputs:
- square: bfloat16 [8192, 8192], P('row', ('col', 'layer'))
The draws below stay inside these ranges and needn't reach their ends.
Inputs may be any that keep to these rules, and one draw needn't show every extreme that they name: `pattern`: every diagonal atom block is stored; blocks near the diagonal are stored more often than far ones.
All inputs are finite; a program needn't handle non-finite values. No bound on the sum of `keep` on one device may be relied on, other than what follows from the above.
Results may differ from the reference program's by a relative error of at most 0.012.
Values may be sent and summed in bfloat16 or wider, within the bound.
No kernel may reach another device: no remote copies, remote signals or barrier semaphores. Data moves between devices by JAX's collectives and lax.ppermute only.
A program may use at most 128 MiB of HBM per device.

```python
import jax
import jax.numpy as jnp
from jax import lax

BLOCK = 32
BPP = 1
N = 8192
NB = 256
N_LAYER = 4


def draw_pattern(key, part):
    key = jax.random.fold_in(key, 7)
    index = jnp.arange(NB)
    distance = jnp.abs(index[:, None] - index[None, :])
    threshold = jnp.where(distance <= 8, 600, jnp.where(distance <= 64, 250, 60))
    rolled = jax.random.randint(key, (NB, NB), 0, 1000)
    return jnp.where((rolled < threshold) | (distance == 0), 1, 0).astype(jnp.int32)


def plant(entries, rng, least, top_value):
    place = [jax.random.randint(jax.random.fold_in(rng, axis), (), 0, length) for axis, length in enumerate(entries.shape)]
    widest = entries.shape.index(max(entries.shape))
    next_to = place[:widest] + [(place[widest] + 1) % entries.shape[widest]] + place[widest + 1:]
    return entries.at[tuple(place)].set(least).at[tuple(next_to)].set(top_value)


def steps_of(stream_key, extent, shards, low, largest):
    def one(position, parts):
        heights = jax.random.uniform(jax.random.fold_in(jax.random.fold_in(stream_key, 6), position), (parts,), jnp.float32, low / len(shards), largest / len(shards))
        return jnp.repeat(jnp.exp(heights), extent[position] // parts).reshape((-1,) + (1,) * (len(extent) - position - 1))

    loudness = one(*shards[0])
    for cut in shards[1:]:
        loudness = loudness * one(*cut)
    return loudness


def bell_draw(key, extent, width, bound, split=(), kind=jnp.bfloat16):
    array = width * jax.random.normal(key, extent, jnp.float32)
    if split:
        array = array * steps_of(key, extent, split, -0.22, 0.18)
    return jnp.clip(array, -bound, bound).astype(kind)


def setup_inputs(seed: int = 0) -> dict:
    keys = jax.random.split(jax.random.key(seed), 4)
    matrix = bell_draw(keys[0], (N, N), 0.2, 1.1953125, ((0, 4), (1, 16)))
    pattern = draw_pattern(jax.random.fold_in(keys[3], 71), 0)
    keep = plant((jax.random.randint(keys[2], (NB, NB), 0, 4) < 3).astype(jnp.int32), jax.random.fold_in(keys[2], 1), 0, 1)
    return {"matrix": matrix, "pattern": pattern, "keep": keep}


def blockwise(values, mask):
    rows, cols = mask.shape
    shaped = values.reshape(rows, BLOCK, cols, BLOCK)
    kept = jnp.where(mask[:, None, :, None] > 0, shaped, jnp.zeros((), values.dtype))
    return kept.reshape(rows * BLOCK, cols * BLOCK)


def reference(matrix, pattern, keep):
    sparse = blockwise(matrix, pattern)
    piece = BLOCK * BPP
    groups = N // (piece * N_LAYER)
    left_all = sparse.reshape(N, groups, N_LAYER, piece)
    right_all = sparse.reshape(groups, N_LAYER, piece, N)
    full = jnp.zeros((N, N), jnp.float32)
    for level in range(N_LAYER):
        left = left_all[:, :, level, :].reshape(N, groups * piece)
        right = right_all[:, level, :, :].reshape(groups * piece, N)
        partial_value = jnp.dot(left, right, preferred_element_type=jnp.float32).astype(jnp.bfloat16)
        partial_value = lax.optimization_barrier(partial_value)
        full = full + partial_value.astype(jnp.float32)
    return blockwise(full, keep).astype(jnp.bfloat16)
```

```python
import functools

import jax
import jax.numpy as jnp
from jax import lax
from jax.experimental import pallas as pl
from jax.experimental.pallas import tpu as pltpu
from jax.sharding import PartitionSpec as P

BLOCK = 32
F32 = jnp.float32
BF16 = jnp.bfloat16
HBM = pl.BlockSpec(memory_space=pl.ANY)
VM = pl.BlockSpec(memory_space=pltpu.VMEM)
PARAMS = pltpu.CompilerParams(vmem_limit_bytes=48 * 1024 * 1024)


def place():
    layer = lax.axis_index("layer")
    return layer // 2, layer % 2


def widen(mask, width):
    k = mask.shape[1]
    rep = lax.broadcasted_iota(jnp.int32, (k, width), 1) // (width // k)
    one = lax.broadcasted_iota(jnp.int32, (k, width), 0)
    spread = jnp.where(rep == one, 1.0, 0.0).astype(F32)
    flag = jnp.where(mask > 0, 1.0, 0.0).astype(F32)
    return jnp.dot(flag, spread, preferred_element_type=F32)


def tall(flags):
    n, width = flags.shape
    return jnp.broadcast_to(flags.reshape(n, 1, width), (n, BLOCK, width)).reshape(
        n * BLOCK, width
    )


def left_kernel(x_ref, pat_ref, s_ref, t_ref, wide, buf, sem):
    a, b = place()
    rows, cols = buf.shape
    copy = pltpu.make_async_copy(
        x_ref.at[pl.ds(pl.multiple_of(a * rows, rows), rows),
                 pl.ds(pl.multiple_of(b * cols, cols), cols)],
        buf, sem)
    copy.start()
    wide[...] = widen(pat_ref[...], wide.shape[1])
    copy.wait()
    atoms = rows // BLOCK
    half = rows // 2
    flags = wide[pl.ds(pl.multiple_of(a * atoms, atoms), atoms),
                 pl.ds(pl.multiple_of(b * cols, cols), cols)]
    s_ref[...] = buf[:half, :] * tall(flags[: atoms // 2]).astype(BF16)
    t_ref[...] = buf[half:, :] * tall(flags[atoms // 2:]).astype(BF16)


def left_blocks(matrix, pattern):
    rows, cols = matrix.shape
    out = jax.ShapeDtypeStruct((rows // 4, cols // 2), BF16)
    return pl.pallas_call(
        left_kernel,
        out_shape=(out, out),
        in_specs=[HBM, VM],
        out_specs=(VM, VM),
        scratch_shapes=[
            pltpu.VMEM((rows // BLOCK, cols), F32),
            pltpu.VMEM((rows // 2, cols // 2), BF16),
            pltpu.SemaphoreType.DMA,
        ],
        compiler_params=PARAMS,
        name="left_blocks",
    )(matrix, pattern)


def right_kernel(x_ref, pat_ref, own_ref, send_ref, wide, buf, sems):
    _, b = place()
    h = lax.axis_index("col") % 2
    cols = wide.shape[1]
    slab = cols // 2
    atoms = slab // BLOCK
    copies = []
    for c in range(4):
        copies.append(pltpu.make_async_copy(
            x_ref.at[pl.ds(pl.multiple_of(c * cols + b * slab, slab), slab), :],
            buf.at[c], sems.at[c]))
        copies[-1].start()
    wide[...] = widen(pat_ref[...], cols)
    for c in range(4):
        copies[c].wait()
        start = pl.multiple_of(c * 2 * atoms + b * atoms, atoms)
        buf[c] = buf[c] * tall(wide[pl.ds(start, atoms), :]).astype(BF16)
    for i in range(2):
        own_ref[i * slab:(i + 1) * slab, :] = buf[2 * i + h]
        send_ref[i * slab:(i + 1) * slab, :] = buf[2 * i + 1 - h]


def right_blocks(matrix, pattern):
    rows, cols = matrix.shape
    out = jax.ShapeDtypeStruct((cols, cols), BF16)
    return pl.pallas_call(
        right_kernel,
        out_shape=(out, out),
        in_specs=[HBM, VM],
        out_specs=(VM, VM),
        scratch_shapes=[
            pltpu.VMEM((rows // BLOCK, cols), F32),
            pltpu.VMEM((4, cols // 2, cols), BF16),
            pltpu.SemaphoreType.DMA((4,)),
        ],
        compiler_params=PARAMS,
        name="right_blocks",
    )(matrix, pattern)


def product_kernel(slot, left_from, right_from, *refs):
    n_left = len(left_from)
    lefts = refs[:n_left]
    rights = refs[n_left:n_left + len(right_from)]
    out_ref, left, right, lsem, rsem = refs[n_left + len(right_from):]
    z = lax.axis_index("col") // 2
    r = lax.axis_index("row")
    half, width = lefts[0].shape
    copies = []
    for i, (step, part) in enumerate(right_from):
        source = lax.rem(r - step + 8, 4)
        depth = rights[i].shape[-2]
        src = rights[i] if part is None else rights[i].at[part]
        copies.append(pltpu.make_async_copy(
            src, right.at[pl.ds(pl.multiple_of(source * depth, depth), depth), :], rsem.at[i]))
    for i, (step, part) in enumerate(left_from):
        source = lax.rem(z - step + 16, 8)
        copies.append(pltpu.make_async_copy(
            lefts[i],
            left.at[pl.ds(part * half, half), pl.ds(pl.multiple_of(source * width, width), width)],
            lsem.at[i]))
    for copy in copies:
        copy.start()
    for copy in copies:
        copy.wait()
    for part in range(2):
        out_ref[part * half:(part + 1) * half, :] = jnp.dot(
            left[part * half:(part + 1) * half, :], right[...], preferred_element_type=F32
        ).astype(out_ref.dtype)


def product(slot, lefts, rights, dtype):
    half, width = lefts[0][0].shape
    depth, cols = rights[0][0].shape[-2:]
    return pl.pallas_call(
        functools.partial(product_kernel, slot, [x[1:] for x in lefts], [x[1:] for x in rights]),
        out_shape=jax.ShapeDtypeStruct((2 * half, cols), dtype),
        in_specs=[HBM] * (len(lefts) + len(rights)),
        out_specs=VM,
        scratch_shapes=[
            pltpu.VMEM((2 * half, 8 * width), BF16),
            pltpu.VMEM((4 * depth, cols), BF16),
            pltpu.SemaphoreType.DMA((len(lefts),)),
            pltpu.SemaphoreType.DMA((len(rights),)),
        ],
        compiler_params=PARAMS,
        name="product%d" % slot,
    )(*[x[0] for x in lefts], *[x[0] for x in rights])


def pieces_kernel(own_ref, other_ref, *outs):
    layer = lax.axis_index("layer")
    width = outs[0].shape[1]
    for d, out in enumerate(outs):
        cols = pl.ds(pl.multiple_of(lax.rem(layer + d, 4) * width, width), width)
        out[...] = (own_ref[:, cols] + other_ref[:, cols].astype(F32)).astype(out.dtype)


def pieces(own, other):
    rows, cols = own.shape
    return pl.pallas_call(
        pieces_kernel,
        out_shape=(jax.ShapeDtypeStruct((rows, cols // 4), BF16),) * 4,
        in_specs=[VM, VM],
        out_specs=(VM,) * 4,
        compiler_params=PARAMS,
        name="pieces",
    )(own, other)


def total_kernel(p0, p1, p2, p3, keep_ref, out_ref, parts, sems):
    layer = lax.axis_index("layer")
    copies = []
    for d, ref in enumerate((p0, p1, p2, p3)):
        copies.append(pltpu.make_async_copy(ref, parts.at[lax.rem(layer - d + 4, 4)], sems.at[d]))
        copies[-1].start()
    flags = widen(keep_ref[...], out_ref.shape[1])
    for copy in copies:
        copy.wait()
    rows = parts.shape[1]
    for a in range(2):
        both = parts[2 * a].astype(F32) + parts[2 * a + 1].astype(F32)
        kept = tall(flags[a * (rows // BLOCK):(a + 1) * (rows // BLOCK)]) > 0.5
        out_ref[a * rows:(a + 1) * rows, :] = jnp.where(kept, both, 0.0).astype(BF16)


def total(parts, keep):
    rows, width = parts[0].shape
    return pl.pallas_call(
        total_kernel,
        out_shape=jax.ShapeDtypeStruct((2 * rows, width), BF16),
        in_specs=[HBM] * 4 + [VM],
        out_specs=VM,
        scratch_shapes=[pltpu.VMEM((4, rows, width), BF16), pltpu.SemaphoreType.DMA((4,))],
        compiler_params=PARAMS,
        name="total",
    )(*parts, keep)


def along_z(x, d):
    return lax.ppermute(x, "col", [(c, (c // 2 + d) % 8 * 2 + c % 2) for c in range(16)])


def along(x, axis, d):
    return lax.ppermute(x, axis, [(i, (i + d) % 4) for i in range(4)])


def swap(x):
    return lax.ppermute(x, "col", [(c, c ^ 1) for c in range(16)])


def on_device(matrix, pattern, keep):
    s, t = left_blocks(matrix, pattern)
    lefts = [(s, 0, 0), (t, 0, 1)]
    s_up = s_down = s
    t_up = t_down = t
    for step in range(1, 5):
        s_up = along_z(s_up, 1)
        lefts.append((s_up, step, 0))
        t_down = along_z(t_down, -1)
        lefts.append((t_down, -step, 1))
        if step < 4:
            t_up = along_z(t_up, 1)
            lefts.append((t_up, step, 1))
            s_down = along_z(s_down, -1)
            lefts.append((s_down, -step, 0))

    mine, theirs = right_blocks(matrix, pattern)
    both = jnp.stack([mine, swap(theirs)])
    below = along(both, "row", 1)
    above = along(both, "row", -1)
    far = [along(below[0], "row", 1), along(above[1], "row", -1)]

    def rights(slot):
        return [(both, 0, slot), (below, 1, slot), (above, -1, slot), (far[slot], 2, None)]

    other = swap(product(1, lefts, rights(1), BF16))
    own = product(0, lefts, rights(0), F32)
    parts = list(pieces(own, other))
    for d in range(1, 4):
        parts[d] = along(parts[d], "layer", d)
    return total(parts, keep)


def solution(mesh):
    in_specs = (P("row", "col"), P("row", "col"), P("row", ("col", "layer")))
    out_specs = P("row", ("col", "layer"))
    return jax.shard_map(
        on_device, mesh=mesh, in_specs=in_specs, out_specs=out_specs, check_vma=False
    )
```

```python
import functools

import jax
import jax.numpy as jnp
from jax import lax
from jax.experimental import pallas as pl
from jax.experimental.pallas import tpu as pltpu
from jax.sharding import PartitionSpec as P

BLOCK = 32
F32 = jnp.float32
BF16 = jnp.bfloat16
ANY = pl.BlockSpec(memory_space=pl.ANY)
HBM = pl.BlockSpec(memory_space=pltpu.HBM)
VM = pl.BlockSpec(memory_space=pltpu.VMEM)


def vmem(mib):
    return pltpu.CompilerParams(vmem_limit_bytes=mib * 1024 * 1024)


def place():
    layer = lax.axis_index("layer")
    return layer // 2, layer % 2


def widen(mask, width):
    k = mask.shape[0]
    rep = lax.broadcasted_iota(jnp.int32, (k, width), 1) // (width // k)
    one = lax.broadcasted_iota(jnp.int32, (k, width), 0)
    spread = jnp.where(rep == one, 1.0, 0.0).astype(F32)
    flag = jnp.where(mask > 0, 1.0, 0.0).astype(F32)
    return lax.dot_general(flag, spread, (((0,), (0,)), ((), ())), preferred_element_type=F32)


def tall(flags):
    n, width = flags.shape
    return jnp.broadcast_to(flags.reshape(n, 1, width), (n, BLOCK, width)).reshape(
        n * BLOCK, width
    )


def left_kernel(x_ref, pat_ref, s_ref, t_ref, wide, buf, sem):
    a, b = place()
    rows, cols = buf.shape
    copy = pltpu.make_async_copy(
        x_ref.at[pl.ds(pl.multiple_of(a * rows, rows), rows),
                 pl.ds(pl.multiple_of(b * cols, cols), cols)],
        buf, sem)
    copy.start()
    wide[...] = widen(pat_ref[...], wide.shape[1])
    copy.wait()
    atoms = rows // BLOCK
    half = rows // 2
    flags = wide[pl.ds(pl.multiple_of(a * atoms, atoms), atoms),
                 pl.ds(pl.multiple_of(b * cols, cols), cols)]
    s_ref[...] = buf[:half, :] * tall(flags[: atoms // 2]).astype(BF16)
    t_ref[...] = buf[half:, :] * tall(flags[atoms // 2:]).astype(BF16)


def left_blocks(matrix, pattern):
    rows, cols = matrix.shape
    out = jax.ShapeDtypeStruct((rows // 4, cols // 2), BF16)
    return pl.pallas_call(
        left_kernel,
        out_shape=(out, out),
        in_specs=[HBM, VM],
        out_specs=(VM, VM),
        scratch_shapes=[
            pltpu.VMEM((rows // BLOCK, cols), F32),
            pltpu.VMEM((rows // 2, cols // 2), BF16),
            pltpu.SemaphoreType.DMA,
        ],
        compiler_params=vmem(6),
        name="left_blocks",
    )(matrix, pattern)


def right_kernel(x_ref, pat_ref, own_ref, send_ref, wide, buf, sems):
    _, b = place()
    h = lax.axis_index("col") % 2
    cols = wide.shape[1]
    slab = cols // 2
    atoms = slab // BLOCK
    copies = []
    for c in range(4):
        copies.append(pltpu.make_async_copy(
            x_ref.at[pl.ds(pl.multiple_of(c * cols + b * slab, slab), slab), :],
            buf.at[c], sems.at[c]))
        copies[-1].start()
    wide[...] = widen(pat_ref[...], cols)
    for c in range(4):
        copies[c].wait()
        start = pl.multiple_of(c * 2 * atoms + b * atoms, atoms)
        buf[c] = buf[c] * tall(wide[pl.ds(start, atoms), :]).astype(BF16)
    for i in range(2):
        own_ref[i * slab:(i + 1) * slab, :] = buf[2 * i + h]
        send_ref[i * slab:(i + 1) * slab, :] = buf[2 * i + 1 - h]


def right_blocks(matrix, pattern):
    rows, cols = matrix.shape
    out = jax.ShapeDtypeStruct((cols, cols), BF16)
    return pl.pallas_call(
        right_kernel,
        out_shape=(out, out),
        in_specs=[HBM, VM],
        out_specs=(VM, VM),
        scratch_shapes=[
            pltpu.VMEM((rows // BLOCK, cols), F32),
            pltpu.VMEM((4, cols // 2, cols), BF16),
            pltpu.SemaphoreType.DMA((4,)),
        ],
        compiler_params=vmem(10),
        name="right_blocks",
    )(matrix, pattern)


def gather_rows(rights, steps, right, sems):
    z = lax.axis_index("col") // 2
    r = lax.axis_index("row")
    up = 1 - 2 * (lax.axis_index("col") % 2)
    deep = rights[0].shape[1] // 2
    wide = rights[0].shape[2]
    slots = right.shape[1] // wide
    waits = []
    for i, step in enumerate(steps):
        source = lax.rem(z - step + 8, 8)
        away = lax.rem((r - source // 2) * up + 8, 4)
        low = pl.multiple_of(lax.rem(source, 2) * deep, deep)
        for j, ref in enumerate(rights):
            copies = [
                pltpu.make_async_copy(
                    ref.at[slot, pl.ds(low, deep), :],
                    right.at[pl.ds(i * deep, deep), pl.ds((slot if slots > 1 else 0) * wide, wide)],
                    sems.at[i, slot])
                for slot in range(2)
            ]

            @pl.when(away == j)
            def _():
                for copy in copies:
                    copy.start()
        waits.append(copies)
    return waits


def early_kernel(steps, *refs):
    n = len(steps[0])
    lefts = (refs[:n], refs[n:2 * n])
    rights = refs[2 * n:2 * n + 4]
    outs = refs[2 * n + 4:2 * n + 8]
    left, right, lsem, rsem = refs[2 * n + 8:]
    half, width = lefts[0][0].shape
    cols = right.shape[2] // 2
    waits = []
    for part in range(2):
        waits += gather_rows(rights, steps[part], right.at[part], rsem.at[part])
        for i in range(n):
            copy = pltpu.make_async_copy(
                lefts[part][i], left.at[part, :, pl.ds(i * width, width)], lsem.at[part, i])
            copy.start()
            waits.append([copy])
    for copies in waits:
        for copy in copies:
            copy.wait()
    for part in range(2):
        for slot in range(2):
            outs[2 * part + slot][...] = jnp.dot(
                left[part], right[part, :, slot * cols:(slot + 1) * cols],
                preferred_element_type=F32)


def early(lefts, steps, rights):
    half, width = lefts[0].shape
    cols = rights[0].shape[2]
    n = len(steps[0])
    out = jax.ShapeDtypeStruct((half, cols), F32)
    return pl.pallas_call(
        functools.partial(early_kernel, steps),
        out_shape=(out,) * 4,
        in_specs=[ANY] * (len(lefts) + 4),
        out_specs=(VM,) * 4,
        scratch_shapes=[
            pltpu.VMEM((2, half, n * width), BF16),
            pltpu.VMEM((2, n * width, 2 * cols), BF16),
            pltpu.SemaphoreType.DMA((2, n)),
            pltpu.SemaphoreType.DMA((2, n, 2)),
        ],
        compiler_params=vmem(20),
        name="early",
    )(*lefts, *rights)


def late_sum(slot, steps, acc_ref, lefts, rights, right, sems):
    z = lax.axis_index("col") // 2
    r = lax.axis_index("row")
    up = 1 - 2 * (lax.axis_index("col") % 2)
    deep = lefts[0].shape[1]
    waits = []
    for i, step in enumerate(steps):
        source = lax.rem(z - step + 8, 8)
        away = lax.rem((r - source // 2) * up + 8, 4)
        low = pl.multiple_of(lax.rem(source, 2) * deep, deep)
        for j, ref in enumerate(rights):
            copy = pltpu.make_async_copy(
                ref.at[slot, pl.ds(low, deep), :], right.at[pl.ds(i * deep, deep), :], sems.at[i])

            @pl.when(away == j)
            def _():
                copy.start()
        waits.append(copy)
    left = jnp.concatenate([ref[...] for ref in lefts], axis=1)
    for copy in waits:
        copy.wait()
    return acc_ref[...] + jnp.dot(left, right[...], preferred_element_type=F32)


def late_other_kernel(steps, acc_ref, *refs):
    n = len(steps)
    out_ref, right, sems = refs[n + 4:]
    out_ref[...] = late_sum(1, steps, acc_ref, refs[:n], refs[n:n + 4], right, sems).astype(BF16)


def late_other(acc, lefts, steps, rights):
    half, cols = acc.shape
    deep = lefts[0].shape[1]
    return pl.pallas_call(
        functools.partial(late_other_kernel, steps),
        out_shape=jax.ShapeDtypeStruct((half, cols), BF16),
        in_specs=[VM] * (1 + len(lefts)) + [ANY] * 4,
        out_specs=VM,
        scratch_shapes=[
            pltpu.VMEM((len(lefts) * deep, cols), BF16),
            pltpu.SemaphoreType.DMA((len(lefts),)),
        ],
        compiler_params=vmem(8),
        name="late_other",
    )(acc, *lefts, *rights)


def late_own_kernel(steps, acc_ref, other_ref, *refs):
    n = len(steps)
    outs = refs[n + 4:n + 8]
    right, whole, sems = refs[n + 8:]
    whole[...] = other_ref[...].astype(F32) + late_sum(
        0, steps, acc_ref, refs[:n], refs[n:n + 4], right, sems)
    layer = lax.axis_index("layer")
    width = outs[0].shape[1]
    for d, out in enumerate(outs):
        cols = pl.ds(pl.multiple_of(lax.rem(layer + d, 4) * width, width), width)
        out[...] = whole[:, cols].astype(out.dtype)


def late_own(acc, other, lefts, steps, rights):
    half, cols = acc.shape
    deep = lefts[0].shape[1]
    return pl.pallas_call(
        functools.partial(late_own_kernel, steps),
        out_shape=(jax.ShapeDtypeStruct((half, cols // 4), BF16),) * 4,
        in_specs=[VM] * (2 + len(lefts)) + [ANY] * 4,
        out_specs=(VM,) * 4,
        scratch_shapes=[
            pltpu.VMEM((len(lefts) * deep, cols), BF16),
            pltpu.VMEM((half, cols), F32),
            pltpu.SemaphoreType.DMA((len(lefts),)),
        ],
        compiler_params=vmem(8),
        name="late_own",
    )(acc, other, *lefts, *rights)


def total_kernel(*refs):
    pieces, (keep_ref, out_ref, parts, sems) = refs[:8], refs[8:]
    layer = lax.axis_index("layer")
    half = pieces[0].shape[0]
    copies = []
    for part in range(2):
        for d in range(4):
            copies.append(pltpu.make_async_copy(
                pieces[4 * part + d],
                parts.at[lax.rem(layer - d + 4, 4), pl.ds(part * half, half), :],
                sems.at[part, d]))
            copies[-1].start()
    flags = widen(keep_ref[...], out_ref.shape[1])
    for copy in copies:
        copy.wait()
    rows = 2 * half
    for a in range(2):
        both = parts[2 * a].astype(F32) + parts[2 * a + 1].astype(F32)
        kept = tall(flags[a * (rows // BLOCK):(a + 1) * (rows // BLOCK)]) > 0.5
        out_ref[a * rows:(a + 1) * rows, :] = jnp.where(kept, both, 0.0).astype(BF16)


def total(pieces, keep):
    half, width = pieces[0].shape
    return pl.pallas_call(
        total_kernel,
        out_shape=jax.ShapeDtypeStruct((4 * half, width), BF16),
        in_specs=[ANY] * 8 + [VM],
        out_specs=VM,
        scratch_shapes=[
            pltpu.VMEM((4, 2 * half, width), BF16),
            pltpu.SemaphoreType.DMA((2, 4)),
        ],
        compiler_params=vmem(8),
        name="total",
    )(*pieces, keep)


def along_z(x, d):
    return lax.ppermute(x, "col", [(c, (c // 2 + d) % 8 * 2 + c % 2) for c in range(16)])


def along(x, axis, d):
    return lax.ppermute(x, axis, [(i, (i + d) % 4) for i in range(4)])


def swap(x):
    return lax.ppermute(x, "col", [(c, c ^ 1) for c in range(16)])


def turn(x, d):
    pairs = []
    for r in range(4):
        for c in range(16):
            to = (r + (d if c % 2 == 0 else -d)) % 4
            pairs.append((r * 16 + c, to * 16 + c))
    return lax.ppermute(x, ("row", "col"), pairs)


def on_device(matrix, pattern, keep):
    pattern_t = pattern.T
    matrix = pltpu.with_memory_space_constraint(matrix, pltpu.HBM)
    s, t = left_blocks(matrix, pattern_t)
    s, t, matrix, pattern_t = lax.optimization_barrier((s, t, matrix, pattern_t))
    left = ({0: s}, {0: t})
    for step in (1, 2, 3, 4):
        for part in range(2):
            for way in (1, -1):
                if step < 4 or way == (1, -1)[part]:
                    at = way * step
                    left[part][at] = along_z(left[part][at - way], way)

    mine, theirs = right_blocks(matrix, pattern_t)
    both = jnp.stack([mine, swap(theirs)])
    below = turn(both, 1)
    above = turn(both, -1)
    far = turn(below, 1)
    rights = [both, below, far, above]

    order = ((0, 1, -1, 2, -2, 3), (0, -1, 1, -2, 2, -3))
    last = ((-3, 4), (3, -4))
    acc = early([left[p][i] for p in range(2) for i in order[p]], order, rights)
    pieces = []
    for p in range(2):
        blocks = [left[p][i] for i in last[p]]
        other = swap(late_other(acc[2 * p + 1], blocks, last[p], rights))
        mine = late_own(acc[2 * p], other, blocks, last[p], rights)
        pieces += [mine[0]] + [along(mine[d], "layer", d) for d in range(1, 4)]
    return total(pieces, keep.T)


def solution(mesh):
    in_specs = (P("row", "col"), P("row", "col"), P("row", ("col", "layer")))
    out_specs = P("row", ("col", "layer"))
    return jax.shard_map(
        on_device, mesh=mesh, in_specs=in_specs, out_specs=out_specs, check_vma=False
    )
```

```python
import functools

import jax
import jax.numpy as jnp
from jax import lax
from jax.experimental import pallas as pl
from jax.experimental.pallas import tpu as pltpu
from jax.sharding import PartitionSpec as P

BLOCK = 32
F32 = jnp.float32
BF16 = jnp.bfloat16
ANY = pl.BlockSpec(memory_space=pl.ANY)
HBM = pl.BlockSpec(memory_space=pltpu.HBM)
VM = pl.BlockSpec(memory_space=pltpu.VMEM)


def vmem(mib):
    return pltpu.CompilerParams(vmem_limit_bytes=mib * 1024 * 1024)


def place():
    layer = lax.axis_index("layer")
    return layer // 2, layer % 2


def widen(mask, width):
    k = mask.shape[0]
    rep = lax.broadcasted_iota(jnp.int32, (k, width), 1) // (width // k)
    one = lax.broadcasted_iota(jnp.int32, (k, width), 0)
    spread = jnp.where(rep == one, 1.0, 0.0).astype(F32)
    flag = jnp.where(mask > 0, 1.0, 0.0).astype(F32)
    return lax.dot_general(flag, spread, (((0,), (0,)), ((), ())), preferred_element_type=F32)


def tall(flags):
    n, width = flags.shape
    return jnp.broadcast_to(flags.reshape(n, 1, width), (n, BLOCK, width)).reshape(
        n * BLOCK, width
    )


def left_kernel(x_ref, pat_ref, out_ref, wide, buf, sem):
    a, b = place()
    rows, cols = buf.shape
    copy = pltpu.make_async_copy(
        x_ref.at[pl.ds(pl.multiple_of(a * rows, rows), rows),
                 pl.ds(pl.multiple_of(b * cols, cols), cols)],
        buf, sem)
    copy.start()
    wide[...] = widen(pat_ref[...], wide.shape[1])
    copy.wait()
    atoms = rows // BLOCK
    flags = wide[pl.ds(pl.multiple_of(a * atoms, atoms), atoms),
                 pl.ds(pl.multiple_of(b * cols, cols), cols)]
    out_ref[...] = buf[...] * tall(flags).astype(BF16)


def left_blocks(matrix, pattern):
    rows, cols = matrix.shape
    return pl.pallas_call(
        left_kernel,
        out_shape=jax.ShapeDtypeStruct((rows // 2, cols // 2), BF16),
        in_specs=[HBM, VM],
        out_specs=VM,
        scratch_shapes=[
            pltpu.VMEM((rows // BLOCK, cols), F32),
            pltpu.VMEM((rows // 2, cols // 2), BF16),
            pltpu.SemaphoreType.DMA,
        ],
        compiler_params=vmem(6),
        name="left_blocks",
    )(matrix, pattern)


def right_kernel(x_ref, pat_ref, own_ref, send_ref, wide, buf, sems):
    _, b = place()
    h = lax.axis_index("col") % 2
    cols = wide.shape[1]
    slab = cols // 2
    atoms = slab // BLOCK
    copies = []
    for c in range(4):
        copies.append(pltpu.make_async_copy(
            x_ref.at[pl.ds(pl.multiple_of(c * cols + b * slab, slab), slab), :],
            buf.at[c], sems.at[c]))
        copies[-1].start()
    wide[...] = widen(pat_ref[...], cols)
    for c in range(4):
        copies[c].wait()
        start = pl.multiple_of(c * 2 * atoms + b * atoms, atoms)
        buf[c] = buf[c] * tall(wide[pl.ds(start, atoms), :]).astype(BF16)
    for i in range(2):
        own_ref[i * slab:(i + 1) * slab, :] = buf[2 * i + h]
        send_ref[i * slab:(i + 1) * slab, :] = buf[2 * i + 1 - h]


def right_blocks(matrix, pattern):
    rows, cols = matrix.shape
    out = jax.ShapeDtypeStruct((cols, cols), BF16)
    return pl.pallas_call(
        right_kernel,
        out_shape=(out, out),
        in_specs=[HBM, VM],
        out_specs=(VM, VM),
        scratch_shapes=[
            pltpu.VMEM((rows // BLOCK, cols), F32),
            pltpu.VMEM((4, cols // 2, cols), BF16),
            pltpu.SemaphoreType.DMA((4,)),
        ],
        compiler_params=vmem(10),
        name="right_blocks",
    )(matrix, pattern)


def side():
    return 1 - 2 * (lax.axis_index("col") % 2)


def gather_rows(rights, steps, slots, right, sems):
    z = lax.axis_index("col") // 2
    r = lax.axis_index("row")
    deep = rights[0].shape[1] // 2
    wide = rights[0].shape[2]
    waits = []
    for i, step in enumerate(steps):
        source = lax.rem(z - step * side() + 8, 8)
        away = lax.rem((r - source // 2) * side() + 8, 4)
        low = pl.multiple_of(lax.rem(source, 2) * deep, deep)
        for j, ref in enumerate(rights):
            copies = [
                pltpu.make_async_copy(
                    ref.at[slot, pl.ds(low, deep), :],
                    right.at[pl.ds(i * deep, deep), pl.ds(k * wide, wide)],
                    sems.at[i, k])
                for k, slot in enumerate(slots)
            ]

            @pl.when(away == j)
            def _():
                for copy in copies:
                    copy.start()
        waits += copies
    return waits


def early_kernel(steps, *refs):
    n = len(steps)
    lefts, rights, outs = refs[:n], refs[n:n + 4], refs[n + 4:n + 8]
    left, right, lsem, rsem = refs[n + 8:]
    half, cols = outs[0].shape
    width = lefts[0].shape[1]
    waits = gather_rows(rights, steps, (0, 1), right, rsem)
    for i in range(n):
        waits.append(pltpu.make_async_copy(
            lefts[i], left.at[:, pl.ds(i * width, width)], lsem.at[i]))
        waits[-1].start()
    for copy in waits:
        copy.wait()
    for part in range(2):
        for slot in range(2):
            outs[2 * part + slot][...] = jnp.dot(
                left[part * half:(part + 1) * half, :],
                right[:, slot * cols:(slot + 1) * cols],
                preferred_element_type=F32)


def early(lefts, steps, rights):
    rows, width = lefts[0].shape
    cols = rights[0].shape[2]
    n = len(steps)
    out = jax.ShapeDtypeStruct((rows // 2, cols), F32)
    return pl.pallas_call(
        functools.partial(early_kernel, steps),
        out_shape=(out,) * 4,
        in_specs=[ANY] * (n + 4),
        out_specs=(VM,) * 4,
        scratch_shapes=[
            pltpu.VMEM((rows, n * width), BF16),
            pltpu.VMEM((n * width, 2 * cols), BF16),
            pltpu.SemaphoreType.DMA((n,)),
            pltpu.SemaphoreType.DMA((n, 2)),
        ],
        compiler_params=vmem(16),
        name="early",
    )(*lefts, *rights)


def late_sum(slot, steps, acc_ref, lefts, rights, right, sems):
    waits = gather_rows(rights, steps, (slot,), right, sems)
    left = jnp.concatenate([ref[...] for ref in lefts], axis=1)
    for copy in waits:
        copy.wait()
    return acc_ref[...] + jnp.dot(left, right[...], preferred_element_type=F32)


def late_other_kernel(steps, acc_ref, *refs):
    n = len(steps)
    out_ref, right, sems = refs[n + 4:]
    out_ref[...] = late_sum(1, steps, acc_ref, refs[:n], refs[n:n + 4], right, sems).astype(BF16)


def late_other(acc, lefts, steps, rights):
    half, cols = acc.shape
    deep = lefts[0].shape[1]
    return pl.pallas_call(
        functools.partial(late_other_kernel, steps),
        out_shape=jax.ShapeDtypeStruct((half, cols), BF16),
        in_specs=[VM] * (1 + len(lefts)) + [ANY] * 4,
        out_specs=VM,
        scratch_shapes=[
            pltpu.VMEM((len(lefts) * deep, cols), BF16),
            pltpu.SemaphoreType.DMA((len(lefts), 1)),
        ],
        compiler_params=vmem(8),
        name="late_other",
    )(acc, *lefts, *rights)


def late_own_kernel(steps, acc_ref, other_ref, *refs):
    n = len(steps)
    outs = refs[n + 4:n + 8]
    right, whole, sems = refs[n + 8:]
    whole[...] = other_ref[...].astype(F32) + late_sum(
        0, steps, acc_ref, refs[:n], refs[n:n + 4], right, sems)
    layer = lax.axis_index("layer")
    width = outs[0].shape[1]
    for d, out in enumerate(outs):
        cols = pl.ds(pl.multiple_of(lax.rem(layer + d, 4) * width, width), width)
        out[...] = whole[:, cols].astype(out.dtype)


def late_own(acc, other, lefts, steps, rights):
    half, cols = acc.shape
    deep = lefts[0].shape[1]
    return pl.pallas_call(
        functools.partial(late_own_kernel, steps),
        out_shape=(jax.ShapeDtypeStruct((half, cols // 4), BF16),) * 4,
        in_specs=[VM] * (2 + len(lefts)) + [ANY] * 4,
        out_specs=(VM,) * 4,
        scratch_shapes=[
            pltpu.VMEM((len(lefts) * deep, cols), BF16),
            pltpu.VMEM((half, cols), F32),
            pltpu.SemaphoreType.DMA((len(lefts), 1)),
        ],
        compiler_params=vmem(8),
        name="late_own",
    )(acc, other, *lefts, *rights)


def total_kernel(*refs):
    pieces, (keep_ref, out_ref, parts, sems) = refs[:8], refs[8:]
    layer = lax.axis_index("layer")
    half = pieces[0].shape[0]
    copies = []
    for part in range(2):
        for d in range(4):
            copies.append(pltpu.make_async_copy(
                pieces[4 * part + d],
                parts.at[lax.rem(layer - d + 4, 4), pl.ds(part * half, half), :],
                sems.at[part, d]))
            copies[-1].start()
    flags = widen(keep_ref[...], out_ref.shape[1])
    for copy in copies:
        copy.wait()
    rows = 2 * half
    for a in range(2):
        both = parts[2 * a].astype(F32) + parts[2 * a + 1].astype(F32)
        kept = tall(flags[a * (rows // BLOCK):(a + 1) * (rows // BLOCK)]) > 0.5
        out_ref[a * rows:(a + 1) * rows, :] = jnp.where(kept, both, 0.0).astype(BF16)


def total(pieces, keep):
    half, width = pieces[0].shape
    return pl.pallas_call(
        total_kernel,
        out_shape=jax.ShapeDtypeStruct((4 * half, width), BF16),
        in_specs=[ANY] * 8 + [VM],
        out_specs=VM,
        scratch_shapes=[
            pltpu.VMEM((4, 2 * half, width), BF16),
            pltpu.SemaphoreType.DMA((2, 4)),
        ],
        compiler_params=vmem(8),
        name="total",
    )(*pieces, keep)


def stream(x, d):
    return lax.ppermute(
        x, "col", [(c, (c // 2 + (d if c % 2 == 0 else -d)) % 8 * 2 + c % 2) for c in range(16)])


def along(x, axis, d):
    return lax.ppermute(x, axis, [(i, (i + d) % 4) for i in range(4)])


def swap(x):
    return lax.ppermute(x, "col", [(c, c ^ 1) for c in range(16)])


def turn(x, d):
    pairs = []
    for r in range(4):
        for c in range(16):
            to = (r + (d if c % 2 == 0 else -d)) % 4
            pairs.append((r * 16 + c, to * 16 + c))
    return lax.ppermute(x, ("row", "col"), pairs)


def on_device(matrix, pattern, keep):
    pattern_t = pattern.T
    matrix = pltpu.with_memory_space_constraint(matrix, pltpu.HBM)
    block = left_blocks(matrix, pattern_t)
    block, matrix, pattern_t = lax.optimization_barrier((block, matrix, pattern_t))
    mine, theirs = right_blocks(matrix, pattern_t)
    both = jnp.stack([mine, swap(theirs)])

    up, down = stream(block, 1), stream(block, -1)
    near = turn(both, 1)
    blocks = {0: block, 1: up, -1: down}
    up, down, both = lax.optimization_barrier((up, down, both))
    up, down, other = stream(up, 1), stream(down, -1), turn(both, -1)
    blocks.update({2: up, -2: down})
    up, down, near = lax.optimization_barrier((up, down, near))
    far = turn(near, 1)
    up, down = stream(up, 1), stream(down, -1)
    blocks.update({3: up, -3: down})
    up, down, other, far = lax.optimization_barrier((up, down, other, far))
    half = up.shape[0] // 2
    ends = [stream(up[p * half:(p + 1) * half], 1) for p in range(2)]
    rights = [both, near, far, other]

    first, last = (0, 1, -1, 2, -2, 3, -3), (4,)
    acc = early([blocks[i] for i in first], first, rights)
    pieces = []
    for p in range(2):
        other = swap(late_other(acc[2 * p + 1], [ends[p]], last, rights))
        mine = late_own(acc[2 * p], other, [ends[p]], last, rights)
        pieces += [mine[0]] + [along(mine[d], "layer", d) for d in range(1, 4)]
    return total(pieces, keep.T)


def solution(mesh):
    in_specs = (P("row", "col"), P("row", "col"), P("row", ("col", "layer")))
    out_specs = P("row", ("col", "layer"))
    return jax.shard_map(
        on_device, mesh=mesh, in_specs=in_specs, out_specs=out_specs, check_vma=False
    )
```

```python
import functools

import jax
import jax.numpy as jnp
from jax import lax
from jax.experimental import pallas as pl
from jax.experimental.pallas import tpu as pltpu
from jax.sharding import PartitionSpec as P

BLOCK = 32
F32 = jnp.float32
BF16 = jnp.bfloat16
ANY = pl.BlockSpec(memory_space=pl.ANY)
HBM = pl.BlockSpec(memory_space=pltpu.HBM)
VM = pl.BlockSpec(memory_space=pltpu.VMEM)


def vmem(mib):
    return pltpu.CompilerParams(vmem_limit_bytes=mib * 1024 * 1024)


def place():
    layer = lax.axis_index("layer")
    return layer // 2, layer % 2


def widen(mask, width):
    k = mask.shape[0]
    rep = lax.broadcasted_iota(jnp.int32, (k, width), 1) // (width // k)
    one = lax.broadcasted_iota(jnp.int32, (k, width), 0)
    spread = jnp.where(rep == one, 1.0, 0.0).astype(F32)
    flag = jnp.where(mask > 0, 1.0, 0.0).astype(F32)
    return lax.dot_general(flag, spread, (((0,), (0,)), ((), ())), preferred_element_type=F32)


def tall(flags):
    n, width = flags.shape
    return jnp.broadcast_to(flags.reshape(n, 1, width), (n, BLOCK, width)).reshape(
        n * BLOCK, width
    )


def prepare_kernel(x_ref, pat_ref, left_ref, own_ref, send_ref, pat, wide, buf, slabs, sems):
    a, b = place()
    h = lax.axis_index("col") % 2
    rows, cols = buf.shape
    copies = [
        pltpu.make_async_copy(pat_ref, pat, sems.at[0]),
        pltpu.make_async_copy(
            x_ref.at[pl.ds(pl.multiple_of(a * rows, rows), rows),
                     pl.ds(pl.multiple_of(b * cols, cols), cols)],
            buf, sems.at[1]),
    ]
    for c in range(4):
        copies.append(pltpu.make_async_copy(
            x_ref.at[pl.ds(pl.multiple_of((2 * c + b) * cols, cols), cols), :],
            slabs.at[c], sems.at[2 + c]))
    for copy in copies:
        copy.start()
    copies[0].wait()
    wide[...] = widen(pat[...], wide.shape[1])
    copies[1].wait()
    atoms = rows // BLOCK
    flags = wide[pl.ds(pl.multiple_of(a * atoms, atoms), atoms),
                 pl.ds(pl.multiple_of(b * cols, cols), cols)]
    left_ref[...] = buf[...] * tall(flags).astype(BF16)
    atoms = cols // BLOCK
    for copy in copies[2:]:
        copy.wait()
    for i in range(2):
        for ref, k in ((own_ref, 2 * i + h), (send_ref, 2 * i + 1 - h)):
            at = pl.ds(pl.multiple_of((2 * k + b) * atoms, atoms), atoms)
            ref[i * cols:(i + 1) * cols, :] = slabs[k] * tall(wide[at, :]).astype(BF16)


def prepare(matrix, pattern_t):
    rows, cols = matrix.shape
    right = jax.ShapeDtypeStruct((cols, cols), BF16)
    return pl.pallas_call(
        prepare_kernel,
        out_shape=(jax.ShapeDtypeStruct((rows // 2, cols // 2), BF16), right, right),
        in_specs=[HBM, HBM],
        out_specs=(VM,) * 3,
        scratch_shapes=[
            pltpu.VMEM(pattern_t.shape, jnp.int32),
            pltpu.VMEM((rows // BLOCK, cols), F32),
            pltpu.VMEM((rows // 2, cols // 2), BF16),
            pltpu.VMEM((4, cols // 2, cols), BF16),
            pltpu.SemaphoreType.DMA((6,)),
        ],
        compiler_params=vmem(12),
        name="prepare",
    )(matrix, pattern_t)


def side():
    return 1 - 2 * (lax.axis_index("col") % 2)


def meeting(step):
    source = lax.rem(lax.axis_index("col") // 2 - step * side() + 8, 8)
    away = lax.rem((lax.axis_index("row") - source // 2) * side() + 8, 4)
    return away, lax.rem(source, 2)


def early_kernel(steps, *refs):
    n = len(steps)
    lefts, (own, near, other), outs = refs[:n], refs[n:n + 3], refs[n + 3:n + 7]
    left, right, lsem, rsem = refs[n + 7:]
    half, cols = outs[0].shape
    width = lefts[0].shape[1]
    waits = []
    for i, step in enumerate(steps):
        away, low = meeting(step)
        low = pl.multiple_of(low * width, width)
        copy = pltpu.make_async_copy(lefts[i], left.at[:, pl.ds(i * width, width)], lsem.at[i])
        waits.append((copy, away != 2))
        pl.when(away != 2)(copy.start)

        @pl.when(away == 2)
        def _():
            left[:, i * width:(i + 1) * width] = jnp.zeros((2 * half, width), BF16)

        for ref, here in ((own, (away == 0) | (away == 2)), (near, away == 1), (other, away == 3)):
            for slot in range(2):
                copy = pltpu.make_async_copy(
                    ref.at[slot, pl.ds(low, width), :],
                    right.at[pl.ds(i * width, width), pl.ds(slot * cols, cols)],
                    rsem.at[i, slot])
                waits.append((copy, here))
                pl.when(here)(copy.start)
    for copy, here in waits:
        pl.when(here)(copy.wait)
    for part in range(2):
        for slot in range(2):
            outs[2 * part + slot][...] = jnp.dot(
                left[part * half:(part + 1) * half, :],
                right[:, slot * cols:(slot + 1) * cols],
                preferred_element_type=F32)


def early(lefts, steps, rights):
    rows, width = lefts[0].shape
    cols = rights[0].shape[2]
    n = len(steps)
    out = jax.ShapeDtypeStruct((rows // 2, cols), F32)
    return pl.pallas_call(
        functools.partial(early_kernel, steps),
        out_shape=(out,) * 4,
        in_specs=[ANY] * (n + 3),
        out_specs=(VM,) * 4,
        scratch_shapes=[
            pltpu.VMEM((rows, n * width), BF16),
            pltpu.VMEM((n * width, 2 * cols), BF16),
            pltpu.SemaphoreType.DMA((n,)),
            pltpu.SemaphoreType.DMA((n, 2)),
        ],
        compiler_params=vmem(16),
        name="early",
    )(*lefts, *rights)


def late_sum(part, slot, steps, acc_ref, ends, lefts, rights, left, right, lsem, rsem):
    half, width = acc_ref.shape[0], lefts[0].shape[1]
    z, r = lax.axis_index("col") // 2, lax.axis_index("row")
    rows = pl.ds(part * half, half)
    waits = []

    def copy(source, target, sem, here=None):
        one = pltpu.make_async_copy(source, target, sem)
        if here is None:
            one.start()
            waits.append(one.wait)
        else:
            pl.when(here)(one.start)
            waits.append(lambda: pl.when(here)(one.wait))

    for i, (end, step) in enumerate(zip(ends, (4, -3))):
        away, low = meeting(step)
        low = pl.multiple_of(low * width, width)
        at = pl.ds(i * width, width)
        copy(end.at[rows, :], left.at[:, at], lsem.at[i])
        for j, ref in enumerate(rights):
            copy(ref.at[slot, pl.ds(low, width), :], right.at[at, :], rsem.at[i], away == j)
    copy(rights[2].at[slot], right.at[pl.ds(2 * width, 2 * width), :], rsem.at[2])
    for q in range(2):
        source = 2 * lax.rem(r + 2, 4) + q
        step = lax.rem((z - source) * side() + 16, 8)
        at = pl.ds((2 + q) * width, width)
        for i, ref in enumerate(lefts):
            copy(ref.at[rows, :], left.at[:, at], lsem.at[2 + q], step == steps[i] % 8)

        @pl.when((step == 4) | (step == 5))
        def _():
            left[:, (2 + q) * width:(3 + q) * width] = jnp.zeros((half, width), BF16)

    for wait in waits:
        wait()
    return acc_ref[...] + jnp.dot(left[...], right[...], preferred_element_type=F32)


def late_scratch(half, width, cols):
    return [
        pltpu.VMEM((half, 4 * width), BF16),
        pltpu.VMEM((4 * width, cols), BF16),
        pltpu.SemaphoreType.DMA((4,)),
        pltpu.SemaphoreType.DMA((3,)),
    ]


def late_other_kernel(part, steps, acc_ref, *refs):
    ends, refs = refs[:2], refs[2:]
    n = len(steps)
    out_ref, *scratch = refs[n + 4:]
    out_ref[...] = late_sum(
        part, 1, steps, acc_ref, ends, refs[:n], refs[n:n + 4], *scratch).astype(BF16)


def late_other(part, acc, ends, lefts, steps, rights):
    half, cols = acc.shape
    return pl.pallas_call(
        functools.partial(late_other_kernel, part, steps),
        out_shape=jax.ShapeDtypeStruct((half, cols), BF16),
        in_specs=[VM] + [ANY] * (6 + len(lefts)),
        out_specs=VM,
        scratch_shapes=late_scratch(half, lefts[0].shape[1], cols),
        compiler_params=vmem(8),
        name="late_other",
    )(acc, *ends, *lefts, *rights)


def late_own_kernel(part, steps, acc_ref, other_ref, *refs):
    ends, refs = refs[:2], refs[2:]
    n = len(steps)
    outs, whole, scratch = refs[n + 4:n + 8], refs[n + 8], refs[n + 9:]
    whole[...] = other_ref[...].astype(F32) + late_sum(
        part, 0, steps, acc_ref, ends, refs[:n], refs[n:n + 4], *scratch)
    layer = lax.axis_index("layer")
    width = outs[0].shape[1]
    for d, out in enumerate(outs):
        cols = pl.ds(pl.multiple_of(lax.rem(layer + d, 4) * width, width), width)
        out[...] = whole[:, cols].astype(out.dtype)


def late_own(part, acc, other, ends, lefts, steps, rights):
    half, cols = acc.shape
    return pl.pallas_call(
        functools.partial(late_own_kernel, part, steps),
        out_shape=(jax.ShapeDtypeStruct((half, cols // 4), BF16),) * 4,
        in_specs=[VM] * 2 + [ANY] * (6 + len(lefts)),
        out_specs=(VM,) * 4,
        scratch_shapes=[pltpu.VMEM((half, cols), F32)] + late_scratch(half, lefts[0].shape[1], cols),
        compiler_params=vmem(8),
        name="late_own",
    )(acc, other, *ends, *lefts, *rights)


def total_kernel(part, p0, p1, p2, p3, keep_ref, *refs):
    out_ref, held, sems = refs[-3:]
    pieces = (p0, p1, p2, p3)
    layer = lax.axis_index("layer")
    half, width = p0.shape
    atoms = half // BLOCK
    flags = widen(keep_ref[...], width)
    for value in range(4):

        @pl.when(layer == value)
        def _():
            for a in range(2):
                two = [pieces[(value - 2 * a - b) % 4][...].astype(F32) for b in range(2)]
                at = (2 * a + part) * atoms
                kept = tall(flags[at:at + atoms]) > 0.5
                held[a] = jnp.where(kept, two[0] + two[1], 0.0).astype(BF16)

    copies = [
        pltpu.make_async_copy(
            held.at[a], out_ref.at[pl.ds((2 * a + part) * half, half), :], sems.at[a])
        for a in range(2)
    ]
    for copy in copies:
        copy.start()
    for copy in copies:
        copy.wait()


def total(part, pieces, keep_t, into=None):
    half, width = pieces[0].shape
    more = [] if into is None else [into]
    return pl.pallas_call(
        functools.partial(total_kernel, part),
        out_shape=jax.ShapeDtypeStruct((4 * half, width), BF16),
        in_specs=[VM] * 5 + [HBM] * len(more),
        out_specs=HBM,
        scratch_shapes=[pltpu.VMEM((2, half, width), BF16), pltpu.SemaphoreType.DMA((2,))],
        input_output_aliases={5: 0} if more else {},
        compiler_params=vmem(4),
        name="total",
    )(*pieces, keep_t, *more)


def stream(x, d):
    return lax.ppermute(
        x, "col", [(c, (c // 2 + (d if c % 2 == 0 else -d)) % 8 * 2 + c % 2) for c in range(16)])


def along(x, axis, d):
    return lax.ppermute(x, axis, [(i, (i + d) % 4) for i in range(4)])


def swap(x):
    return lax.ppermute(x, "col", [(c, c ^ 1) for c in range(16)])


def turn(x, d):
    pairs = []
    for r in range(4):
        for c in range(16):
            to = (r + (d if c % 2 == 0 else -d)) % 4
            pairs.append((r * 16 + c, to * 16 + c))
    return lax.ppermute(x, ("row", "col"), pairs)


def after(x, y):
    return lax.optimization_barrier((x, y))[0]


def on_device(matrix, pattern, keep):
    matrix = pltpu.with_memory_space_constraint(matrix, pltpu.HBM)
    pattern_t = pltpu.with_memory_space_constraint(pattern.T, pltpu.HBM)
    block, mine, theirs = prepare(matrix, pattern_t)
    theirs = swap(theirs)
    both = jnp.stack([mine, theirs])

    up1 = stream(block, 1)
    up2 = stream(up1, 1)
    up3 = stream(up2, 1)
    up4 = stream(up3, 1)
    down1 = stream(after(block, theirs), -1)
    down2 = stream(down1, -1)
    down3 = stream(down2, -1)
    near, other = turn(both, 1), turn(both, -1)
    far = turn(after(near, up2), 1)
    rights = [both, near, far, other]

    steps = (0, 1, -1, 2, -2, 3)
    lefts, ends = [block, up1, down1, up2, down2, up3], [up4, down3]
    acc = early(lefts, steps, [both, near, other])
    out, keep_t = None, keep.T
    for p in range(2):
        other = swap(late_other(p, acc[2 * p + 1], ends, lefts, steps, rights))
        mine = late_own(p, acc[2 * p], other, ends, lefts, steps, rights)
        moved = [mine[0]] + [along(mine[d], "layer", d) for d in range(1, 4)]
        out = total(p, moved, keep_t, out)
    return out


def solution(mesh):
    in_specs = (P("row", "col"), P("row", "col"), P("row", ("col", "layer")))
    out_specs = P("row", ("col", "layer"))
    return jax.shard_map(
        on_device, mesh=mesh, in_specs=in_specs, out_specs=out_specs, check_vma=False
    )
```

```python
import functools

import jax
import jax.numpy as jnp
from jax import lax
from jax.experimental import pallas as pl
from jax.experimental.pallas import tpu as pltpu
from jax.sharding import PartitionSpec as P

BLOCK = 32
F32 = jnp.float32
BF16 = jnp.bfloat16
ANY = pl.BlockSpec(memory_space=pl.ANY)
HBM = pl.BlockSpec(memory_space=pltpu.HBM)
VM = pl.BlockSpec(memory_space=pltpu.VMEM)


def vmem(mib):
    return pltpu.CompilerParams(vmem_limit_bytes=mib * 1024 * 1024)


def place():
    layer = lax.axis_index("layer")
    return layer // 2, layer % 2


def widen(mask, width):
    k = mask.shape[0]
    rep = lax.broadcasted_iota(jnp.int32, (k, width), 1) // (width // k)
    one = lax.broadcasted_iota(jnp.int32, (k, width), 0)
    spread = jnp.where(rep == one, 1.0, 0.0).astype(F32)
    flag = jnp.where(mask > 0, 1.0, 0.0).astype(F32)
    return lax.dot_general(flag, spread, (((0,), (0,)), ((), ())), preferred_element_type=F32)


def tall(flags):
    n, width = flags.shape
    return jnp.broadcast_to(flags.reshape(n, 1, width), (n, BLOCK, width)).reshape(
        n * BLOCK, width
    )


def prepare_kernel(x_ref, pat_ref, block_ref, top_ref, low_ref, own_ref, send_ref, pat, wide, buf, slabs, sems):
    a, b = place()
    h = lax.axis_index("col") % 2
    rows, cols = buf.shape
    copies = [
        pltpu.make_async_copy(pat_ref, pat, sems.at[0]),
        pltpu.make_async_copy(
            x_ref.at[pl.ds(pl.multiple_of(a * rows, rows), rows),
                     pl.ds(pl.multiple_of(b * cols, cols), cols)],
            buf, sems.at[1]),
    ]
    for c in range(4):
        copies.append(pltpu.make_async_copy(
            x_ref.at[pl.ds(pl.multiple_of((2 * c + b) * cols, cols), cols), :],
            slabs.at[c], sems.at[2 + c]))
    for copy in copies:
        copy.start()
    copies[0].wait()
    wide[...] = widen(pat[...], wide.shape[1])
    copies[1].wait()
    atoms = rows // BLOCK
    flags = wide[pl.ds(pl.multiple_of(a * atoms, atoms), atoms),
                 pl.ds(pl.multiple_of(b * cols, cols), cols)]
    half = rows // 2
    for part, ref in enumerate((top_ref, low_ref)):
        at = slice(part * half, (part + 1) * half)
        kept = buf[at, :] * tall(flags[part * atoms // 2:(part + 1) * atoms // 2]).astype(BF16)
        ref[...] = kept
        block_ref[at, :] = kept
    atoms = cols // BLOCK
    for copy in copies[2:]:
        copy.wait()
    for i in range(2):
        for ref, k in ((own_ref, 2 * i + h), (send_ref, 2 * i + 1 - h)):
            at = pl.ds(pl.multiple_of((2 * k + b) * atoms, atoms), atoms)
            ref[i * cols:(i + 1) * cols, :] = slabs[k] * tall(wide[at, :]).astype(BF16)


def prepare(matrix, pattern_t):
    rows, cols = matrix.shape
    block = jax.ShapeDtypeStruct((rows // 2, cols // 2), BF16)
    left = jax.ShapeDtypeStruct((rows // 4, cols // 2), BF16)
    right = jax.ShapeDtypeStruct((cols, cols), BF16)
    return pl.pallas_call(
        prepare_kernel,
        out_shape=(block, left, left, right, right),
        in_specs=[HBM, HBM],
        out_specs=(VM,) * 5,
        scratch_shapes=[
            pltpu.VMEM(pattern_t.shape, jnp.int32),
            pltpu.VMEM((rows // BLOCK, cols), F32),
            pltpu.VMEM((rows // 2, cols // 2), BF16),
            pltpu.VMEM((4, cols // 2, cols), BF16),
            pltpu.SemaphoreType.DMA((6,)),
        ],
        compiler_params=vmem(12),
        name="prepare",
    )(matrix, pattern_t)


def side():
    return 1 - 2 * (lax.axis_index("col") % 2)


def meeting(step):
    source = lax.rem(lax.axis_index("col") // 2 - step * side() + 8, 8)
    away = lax.rem((lax.axis_index("row") - source // 2) * side() + 8, 4)
    return away, lax.rem(source, 2)


def halves(refs):
    return [refs[i:i + 2] for i in range(0, len(refs), 2)]


def rows_of(ref, half, part):
    return ref if ref.shape[0] == half else ref.at[pl.ds(part * half, half), :]


def early_kernel(steps, *refs):
    n = len(steps)
    lefts, refs = halves(refs[:2 * n]), refs[2 * n:]
    (own, near, other), outs, (left, right, lsem, rsem) = refs[:3], refs[3:5], refs[5:]
    rows, cols = outs[0].shape
    half, width = lefts[0][0].shape
    waits = []
    for i, step in enumerate(steps):
        away, low = meeting(step)
        low = pl.multiple_of(low * width, width)
        for part in range(2):
            copy = pltpu.make_async_copy(
                rows_of(lefts[i][part], half, part),
                left.at[pl.ds(part * half, half), pl.ds(i * width, width)], lsem.at[i, part])
            waits.append((copy, away != 2))
            pl.when(away != 2)(copy.start)

        @pl.when(away == 2)
        def _():
            left[:, i * width:(i + 1) * width] = jnp.zeros((rows, width), BF16)

        for ref, here in ((own, (away == 0) | (away == 2)), (near, away == 1), (other, away == 3)):
            for slot in range(2):
                copy = pltpu.make_async_copy(
                    ref.at[slot, pl.ds(low, width), :],
                    right.at[pl.ds(i * width, width), pl.ds(slot * cols, cols)],
                    rsem.at[i, slot])
                waits.append((copy, here))
                pl.when(here)(copy.start)
    for copy, here in waits:
        pl.when(here)(copy.wait)
    for slot in range(2):
        outs[slot][...] = jnp.dot(
            left[...], right[:, slot * cols:(slot + 1) * cols], preferred_element_type=F32)


def early(lefts, steps, rights):
    rows, width = 2 * lefts[0].shape[0], lefts[0].shape[1]
    cols = rights[0].shape[2]
    n = len(steps)
    out = jax.ShapeDtypeStruct((rows, cols), F32)
    return pl.pallas_call(
        functools.partial(early_kernel, steps),
        out_shape=(out,) * 2,
        in_specs=[ANY] * (2 * n + 3),
        out_specs=(VM,) * 2,
        scratch_shapes=[
            pltpu.VMEM((rows, n * width), BF16),
            pltpu.VMEM((n * width, 2 * cols), BF16),
            pltpu.SemaphoreType.DMA((n, 2)),
            pltpu.SemaphoreType.DMA((n, 2)),
        ],
        compiler_params=vmem(16),
        name="early",
    )(*lefts, *rights)


def middle_kernel(steps, *refs):
    n = len(steps)
    own_ref, other_ref, *end = refs[:4]
    lefts, refs = halves(refs[4:4 + 2 * n]), refs[4 + 2 * n:]
    rights, refs = refs[:3], refs[3:]
    own_out, other_out, rows_out, left_out, right, lsem, rsem = refs
    rows, width = end[0].shape
    half = rows // 2
    cols = own_out.shape[1]
    z, r = lax.axis_index("col") // 2, lax.axis_index("row")
    waits = []

    def copy(source, target, sem, here):
        one = pltpu.make_async_copy(source, target, sem)
        pl.when(here)(one.start)
        waits.append(lambda: pl.when(here)(one.wait))

    for i, (step, ref) in enumerate(((-3, right), (4, rows_out))):
        away, low = meeting(step)
        low = pl.multiple_of(low * width, width)
        for j, source in zip((0, 1, 3), rights):
            for slot in range(2):
                copy(source.at[slot, pl.ds(low, width), :],
                     ref.at[:, pl.ds(slot * cols, cols)], rsem.at[i, slot], away == j)

        @pl.when(away == 2)
        def _():
            ref[...] = jnp.zeros_like(ref)

    for q in range(2):
        source = 2 * lax.rem(r + 2, 4) + q
        step = lax.rem((z - source) * side() + 16, 8)
        at = pl.ds(q * width, width)
        for i, ref in enumerate([*lefts, end]):
            for part in range(2):
                copy(rows_of(ref[part], half, part), left_out.at[pl.ds(part * half, half), at], lsem.at[q, part],
                     step == (*steps, -3)[i] % 8)

        @pl.when(step == 4)
        def _():
            left_out[:, q * width:(q + 1) * width] = jnp.zeros((rows, width), BF16)

    for wait in waits:
        wait()
    for slot, (ref, out) in enumerate(((own_ref, own_out), (other_ref, other_out))):
        for part in range(2):
            at = slice(part * half, (part + 1) * half)
            out[at, :] = ref[at, :] + jnp.dot(
                end[part][at, :], right[:, slot * cols:(slot + 1) * cols],
                preferred_element_type=F32)


def middle(acc, end, lefts, steps, rights):
    rows, width = end[0].shape
    cols = acc[0].shape[1]
    n = len(steps)
    out = jax.ShapeDtypeStruct((rows, cols), F32)
    return pl.pallas_call(
        functools.partial(middle_kernel, steps),
        out_shape=(
            out, out,
            jax.ShapeDtypeStruct((width, 2 * cols), BF16),
            jax.ShapeDtypeStruct((rows, 2 * width), BF16),
        ),
        in_specs=[VM] * 4 + [ANY] * (2 * n + 3),
        out_specs=(VM,) * 4,
        scratch_shapes=[
            pltpu.VMEM((width, 2 * cols), BF16),
            pltpu.SemaphoreType.DMA((2, 2)),
            pltpu.SemaphoreType.DMA((2, 2)),
        ],
        compiler_params=vmem(16),
        name="middle",
    )(*acc, *end, *lefts, *rights)


def columns(ref, ds, base, width):
    layer = lax.axis_index("layer")
    parts = [
        ref[:, pl.ds(pl.multiple_of(base + lax.rem(layer + d, 4) * width, width), width)]
        for d in ds
    ]
    return parts[0] if len(parts) == 1 else jnp.concatenate(parts, axis=1)


def piece(slot, ds, acc_ref, top_ref, low_ref, rows_ref, left_ref, far_ref):
    cols = acc_ref.shape[1]
    width = cols // 4
    away, low = meeting(4)
    deep = rows_ref.shape[0]
    here = pl.ds(pl.multiple_of(low * deep, deep), deep)
    rows = jnp.where(
        away == 2,
        columns(far_ref.at[slot, here, :], ds, 0, width),
        columns(rows_ref, ds, slot * cols, width))
    last = [jnp.dot(ref[...], rows, preferred_element_type=F32) for ref in (top_ref, low_ref)]
    return (
        columns(acc_ref, ds, 0, width)
        + jnp.concatenate(last, axis=0)
        + jnp.dot(left_ref[...], columns(far_ref.at[slot], ds, 0, width), preferred_element_type=F32)
    )


def others_kernel(ds, *refs):
    refs[-1][...] = piece(1, ds, *refs[:-1]).astype(BF16)


def others(ds, acc, late):
    rows, cols = acc.shape
    return pl.pallas_call(
        functools.partial(others_kernel, ds),
        out_shape=jax.ShapeDtypeStruct((rows, cols // 4 * len(ds)), BF16),
        in_specs=[VM] * 6,
        out_specs=VM,
        compiler_params=vmem(6),
        name="others",
    )(acc, *late)


def owns_kernel(ds, *refs):
    (got_ref, *refs), outs = refs[:7], refs[7:]
    width = outs[0].shape[1]
    sums = piece(0, ds, *refs) + got_ref[:, :width * len(ds)].astype(F32)
    for i, out in enumerate(outs):
        out[...] = sums[:, i * width:(i + 1) * width].astype(BF16)


def owns(ds, got, acc, late):
    rows, cols = acc.shape
    return pl.pallas_call(
        functools.partial(owns_kernel, ds),
        out_shape=(jax.ShapeDtypeStruct((rows, cols // 4), BF16),) * len(ds),
        in_specs=[VM] * 7,
        out_specs=(VM,) * len(ds),
        compiler_params=vmem(4),
        name="owns",
    )(got, acc, *late)


def total_kernel(p1, p2, p3, keep_ref, got_ref, *refs):
    *late, out_ref, part = refs
    layer = lax.axis_index("layer")
    rows, width = p1.shape
    atoms = rows // BLOCK
    got = got_ref[:, got_ref.shape[1] - width:].astype(F32)
    part[...] = (piece(0, (0,), *late) + got).astype(BF16)
    pieces = (part, p1, p2, p3)
    flags = widen(keep_ref[...], width)
    for value in range(4):

        @pl.when(layer == value)
        def _():
            for a in range(2):
                two = [pieces[(value - 2 * a - b) % 4][...].astype(F32) for b in range(2)]
                kept = tall(flags[a * atoms:(a + 1) * atoms]) > 0.5
                both = jnp.where(kept, two[0] + two[1], 0.0)
                out_ref[a * rows:(a + 1) * rows, :] = both.astype(BF16)


def total(moved, keep_t, got, acc, late):
    rows, width = moved[0].shape
    return pl.pallas_call(
        total_kernel,
        out_shape=jax.ShapeDtypeStruct((2 * rows, width), BF16),
        in_specs=[VM] * 11,
        out_specs=VM,
        scratch_shapes=[pltpu.VMEM((rows, width), BF16)],
        compiler_params=vmem(8),
        name="total",
    )(*moved, keep_t, got, acc, *late)


def stream(x, d):
    return lax.ppermute(
        x, "col", [(c, (c // 2 + (d if c % 2 == 0 else -d)) % 8 * 2 + c % 2) for c in range(16)])


def along(x, axis, d):
    return lax.ppermute(x, axis, [(i, (i + d) % 4) for i in range(4)])


def swap(x):
    return lax.ppermute(x, "col", [(c, c ^ 1) for c in range(16)])


def turn(x, d):
    pairs = []
    for r in range(4):
        for c in range(16):
            to = (r + (d if c % 2 == 0 else -d)) % 4
            pairs.append((r * 16 + c, to * 16 + c))
    return lax.ppermute(x, ("row", "col"), pairs)


def after(x, y):
    return lax.optimization_barrier((x, y))[0]


def on_device(matrix, pattern, keep):
    matrix = pltpu.with_memory_space_constraint(matrix, pltpu.HBM)
    pattern_t = pltpu.with_memory_space_constraint(pattern.T, pltpu.HBM)
    block, top, low, mine, theirs = prepare(matrix, pattern_t)
    theirs = swap(theirs)
    both = jnp.stack([mine, theirs])

    left = {0: (top, low)}
    down = block
    for step in range(1, 5):
        left[step] = tuple(stream(x, 1) for x in left[step - 1])
        if step < 4:
            down = stream(down, -1)
            left[-step] = (down, down)
    near, other = turn(both, 1), turn(both, -1)
    far = turn(after(near, (left[2], left[-2])), 1)

    steps = (0, 1, -1, 2, -2, 3)
    lefts, rights = [x for step in steps for x in left[step]], [both, near, other]
    acc = early(lefts, steps, rights)
    own, theirs, rows, meet = middle(acc, left[-3], lefts, steps, rights)
    late = [*left[4], rows, meet, far]
    sent = others((1, 3), theirs, late)
    got = swap(others((2, 0), after(theirs, sent), late))
    part1, part3 = owns((1, 3), swap(sent), own, late)
    (part2,) = owns((2,), got, own, late)
    moved = [along(part1, "layer", 1), along(part2, "layer", 2), along(part3, "layer", 3)]
    return total(moved, keep.T, got, own, late)


def solution(mesh):
    in_specs = (P("row", "col"), P("row", "col"), P("row", ("col", "layer")))
    out_specs = P("row", ("col", "layer"))
    return jax.shard_map(
        on_device, mesh=mesh, in_specs=in_specs, out_specs=out_specs, check_vma=False
    )
```

```python
import functools

import jax
import jax.numpy as jnp
from jax import lax
from jax.experimental import pallas as pl
from jax.experimental.pallas import tpu as pltpu
from jax.sharding import PartitionSpec as P

BLOCK = 32
F32 = jnp.float32
BF16 = jnp.bfloat16
ANY = pl.BlockSpec(memory_space=pl.ANY)
HBM = pl.BlockSpec(memory_space=pltpu.HBM)
VM = pl.BlockSpec(memory_space=pltpu.VMEM)


def vmem(mib):
    return pltpu.CompilerParams(vmem_limit_bytes=mib * 1024 * 1024)


def place():
    layer = lax.axis_index("layer")
    return layer // 2, layer % 2


def widen(mask, width):
    k = mask.shape[0]
    rep = lax.broadcasted_iota(jnp.int32, (k, width), 1) // (width // k)
    one = lax.broadcasted_iota(jnp.int32, (k, width), 0)
    spread = jnp.where(rep == one, 1.0, 0.0).astype(F32)
    flag = jnp.where(mask > 0, 1.0, 0.0).astype(F32)
    return lax.dot_general(flag, spread, (((0,), (0,)), ((), ())), preferred_element_type=F32)


def tall(flags):
    n, width = flags.shape
    return jnp.broadcast_to(flags.reshape(n, 1, width), (n, BLOCK, width)).reshape(
        n * BLOCK, width
    )


def prepare_kernel(x_ref, pat_ref, block_ref, top_ref, low_ref, own_ref, send_ref, pat, wide, buf, slabs, sems):
    a, b = place()
    h = lax.axis_index("col") % 2
    rows, cols = buf.shape
    copies = [
        pltpu.make_async_copy(pat_ref, pat, sems.at[0]),
        pltpu.make_async_copy(
            x_ref.at[pl.ds(pl.multiple_of(a * rows, rows), rows),
                     pl.ds(pl.multiple_of(b * cols, cols), cols)],
            buf, sems.at[1]),
    ]
    for c in range(4):
        copies.append(pltpu.make_async_copy(
            x_ref.at[pl.ds(pl.multiple_of((2 * c + b) * cols, cols), cols), :],
            slabs.at[c], sems.at[2 + c]))
    for copy in copies:
        copy.start()
    copies[0].wait()
    wide[...] = widen(pat[...], wide.shape[1])
    copies[1].wait()
    atoms = rows // BLOCK
    flags = wide[pl.ds(pl.multiple_of(a * atoms, atoms), atoms),
                 pl.ds(pl.multiple_of(b * cols, cols), cols)]
    half = rows // 2
    for part, ref in enumerate((top_ref, low_ref)):
        at = slice(part * half, (part + 1) * half)
        kept = buf[at, :] * tall(flags[part * atoms // 2:(part + 1) * atoms // 2]).astype(BF16)
        ref[...] = kept
        block_ref[at, :] = kept
    atoms = cols // BLOCK
    for copy in copies[2:]:
        copy.wait()
    for i in range(2):
        for ref, k in ((own_ref, 2 * i + h), (send_ref, 2 * i + 1 - h)):
            at = pl.ds(pl.multiple_of((2 * k + b) * atoms, atoms), atoms)
            ref[i * cols:(i + 1) * cols, :] = slabs[k] * tall(wide[at, :]).astype(BF16)


def prepare(matrix, pattern_t):
    rows, cols = matrix.shape
    block = jax.ShapeDtypeStruct((rows // 2, cols // 2), BF16)
    left = jax.ShapeDtypeStruct((rows // 4, cols // 2), BF16)
    right = jax.ShapeDtypeStruct((cols, cols), BF16)
    return pl.pallas_call(
        prepare_kernel,
        out_shape=(block, left, left, right, right),
        in_specs=[HBM, HBM],
        out_specs=(VM,) * 5,
        scratch_shapes=[
            pltpu.VMEM(pattern_t.shape, jnp.int32),
            pltpu.VMEM((rows // BLOCK, cols), F32),
            pltpu.VMEM((rows // 2, cols // 2), BF16),
            pltpu.VMEM((4, cols // 2, cols), BF16),
            pltpu.SemaphoreType.DMA((6,)),
        ],
        compiler_params=vmem(12),
        name="prepare",
    )(matrix, pattern_t)


def side():
    return 1 - 2 * (lax.axis_index("col") % 2)


def meeting(step):
    source = lax.rem(lax.axis_index("col") // 2 - step * side() + 8, 8)
    away = lax.rem((lax.axis_index("row") - source // 2) * side() + 8, 4)
    return away, lax.rem(source, 2)


def halves(refs):
    return [refs[i:i + 2] for i in range(0, len(refs), 2)]


def rows_of(ref, half, part):
    return ref if ref.shape[0] == half else ref.at[pl.ds(part * half, half), :]


def early_kernel(steps, *refs):
    n = len(steps)
    lefts, refs = halves(refs[:2 * n]), refs[2 * n:]
    (own, near, other), outs, (left, right, lsem, rsem) = refs[:3], refs[3:5], refs[5:]
    rows, cols = outs[0].shape
    half, width = lefts[0][0].shape
    waits = []
    for i, step in enumerate(steps):
        away, low = meeting(step)
        low = pl.multiple_of(low * width, width)
        for part in range(2):
            copy = pltpu.make_async_copy(
                rows_of(lefts[i][part], half, part),
                left.at[pl.ds(part * half, half), pl.ds(i * width, width)], lsem.at[i, part])
            waits.append((copy, away != 2))
            pl.when(away != 2)(copy.start)

        @pl.when(away == 2)
        def _():
            left[:, i * width:(i + 1) * width] = jnp.zeros((rows, width), BF16)

        for ref, here in ((own, (away == 0) | (away == 2)), (near, away == 1), (other, away == 3)):
            for slot in range(2):
                copy = pltpu.make_async_copy(
                    ref.at[slot, pl.ds(low, width), :],
                    right.at[pl.ds(i * width, width), pl.ds(slot * cols, cols)],
                    rsem.at[i, slot])
                waits.append((copy, here))
                pl.when(here)(copy.start)
    for copy, here in waits:
        pl.when(here)(copy.wait)
    for slot in range(2):
        outs[slot][...] = jnp.dot(
            left[...], right[:, slot * cols:(slot + 1) * cols], preferred_element_type=F32)


def early(lefts, steps, rights):
    rows, width = 2 * lefts[0].shape[0], lefts[0].shape[1]
    cols = rights[0].shape[2]
    n = len(steps)
    out = jax.ShapeDtypeStruct((rows, cols), F32)
    return pl.pallas_call(
        functools.partial(early_kernel, steps),
        out_shape=(out,) * 2,
        in_specs=[ANY] * (2 * n + 3),
        out_specs=(VM,) * 2,
        scratch_shapes=[
            pltpu.VMEM((rows, n * width), BF16),
            pltpu.VMEM((n * width, 2 * cols), BF16),
            pltpu.SemaphoreType.DMA((n, 2)),
            pltpu.SemaphoreType.DMA((n, 2)),
        ],
        compiler_params=vmem(16),
        name="early",
    )(*lefts, *rights)


def middle_kernel(steps, *refs):
    n = len(steps)
    own_ref, other_ref, *end = refs[:4]
    lefts, refs = halves(refs[4:4 + 2 * n]), refs[4 + 2 * n:]
    rights, refs = refs[:3], refs[3:]
    own_out, other_out, rows_out, left_out, right, lsem, rsem = refs
    rows, width = end[0].shape
    half = rows // 2
    cols = own_out.shape[1]
    z, r = lax.axis_index("col") // 2, lax.axis_index("row")
    waits = []

    def copy(source, target, sem, here):
        one = pltpu.make_async_copy(source, target, sem)
        pl.when(here)(one.start)
        waits.append(lambda: pl.when(here)(one.wait))

    for i, (step, ref) in enumerate(((-3, right), (4, rows_out))):
        away, low = meeting(step)
        low = pl.multiple_of(low * width, width)
        for j, source in zip((0, 1, 3), rights):
            for slot in range(2):
                copy(source.at[slot, pl.ds(low, width), :],
                     ref.at[:, pl.ds(slot * cols, cols)], rsem.at[i, slot], away == j)

        @pl.when(away == 2)
        def _():
            ref[...] = jnp.zeros_like(ref)

    for q in range(2):
        source = 2 * lax.rem(r + 2, 4) + q
        step = lax.rem((z - source) * side() + 16, 8)
        at = pl.ds(q * width, width)
        for i, ref in enumerate([*lefts, end]):
            for part in range(2):
                copy(rows_of(ref[part], half, part), left_out.at[pl.ds(part * half, half), at], lsem.at[q, part],
                     step == (*steps, -3)[i] % 8)

        @pl.when(step == 4)
        def _():
            left_out[:, q * width:(q + 1) * width] = jnp.zeros((rows, width), BF16)

    for wait in waits:
        wait()
    for slot, (ref, out) in enumerate(((own_ref, own_out), (other_ref, other_out))):
        for part in range(2):
            at = slice(part * half, (part + 1) * half)
            out[at, :] = ref[at, :] + jnp.dot(
                end[part][at, :], right[:, slot * cols:(slot + 1) * cols],
                preferred_element_type=F32)


def middle(acc, end, lefts, steps, rights):
    rows, width = end[0].shape
    cols = acc[0].shape[1]
    n = len(steps)
    out = jax.ShapeDtypeStruct((rows, cols), F32)
    return pl.pallas_call(
        functools.partial(middle_kernel, steps),
        out_shape=(
            out, out,
            jax.ShapeDtypeStruct((width, 2 * cols), BF16),
            jax.ShapeDtypeStruct((rows, 2 * width), BF16),
        ),
        in_specs=[VM] * 4 + [ANY] * (2 * n + 3),
        out_specs=(VM,) * 4,
        scratch_shapes=[
            pltpu.VMEM((width, 2 * cols), BF16),
            pltpu.SemaphoreType.DMA((2, 2)),
            pltpu.SemaphoreType.DMA((2, 2)),
        ],
        compiler_params=vmem(16),
        name="middle",
    )(*acc, *end, *lefts, *rights)


def columns(ref, ds, base, width):
    layer = lax.axis_index("layer")
    parts = [
        ref[:, pl.ds(pl.multiple_of(base + lax.rem(layer + d, 4) * width, width), width)]
        for d in ds
    ]
    return parts[0] if len(parts) == 1 else jnp.concatenate(parts, axis=1)


def piece(slot, ds, acc_ref, top_ref, low_ref, rows_ref, left_ref, far_ref):
    cols = acc_ref.shape[1]
    width = cols // 4
    away, low = meeting(4)
    deep = rows_ref.shape[0]
    here = pl.ds(pl.multiple_of(low * deep, deep), deep)
    rows = jnp.where(
        away == 2,
        columns(far_ref.at[slot, here, :], ds, 0, width),
        columns(rows_ref, ds, slot * cols, width))
    last = [jnp.dot(ref[...], rows, preferred_element_type=F32) for ref in (top_ref, low_ref)]
    return (
        columns(acc_ref, ds, 0, width)
        + jnp.concatenate(last, axis=0)
        + jnp.dot(left_ref[...], columns(far_ref.at[slot], ds, 0, width), preferred_element_type=F32)
    )


def others_kernel(ds, *refs):
    refs[-1][...] = piece(1, ds, *refs[:-1]).astype(BF16)


def others(ds, acc, late):
    rows, cols = acc.shape
    return pl.pallas_call(
        functools.partial(others_kernel, ds),
        out_shape=jax.ShapeDtypeStruct((rows, cols // 4 * len(ds)), BF16),
        in_specs=[VM] * 6,
        out_specs=VM,
        compiler_params=vmem(6),
        name="others",
    )(acc, *late)


def owns_kernel(ds, *refs):
    (got_ref, *refs), outs = refs[:7], refs[7:]
    width = outs[0].shape[1]
    sums = piece(0, ds, *refs) + got_ref[:, :width * len(ds)].astype(F32)
    half = outs[0].shape[0]
    for i, out in enumerate(outs):
        k, part = i % len(ds), i // len(ds)
        out[...] = sums[part * half:(part + 1) * half, k * width:(k + 1) * width].astype(BF16)


def owns(ds, got, acc, late):
    rows, cols = acc.shape
    return pl.pallas_call(
        functools.partial(owns_kernel, ds),
        out_shape=(jax.ShapeDtypeStruct((rows // 2, cols // 4), BF16),) * (2 * len(ds)),
        in_specs=[VM] * 7,
        out_specs=(VM,) * (2 * len(ds)),
        compiler_params=vmem(4),
        name="owns",
    )(got, acc, *late)


def total_kernel(*refs):
    moved, (keep_ref, got_ref, *late, out_ref, part) = refs[:6], refs[6:]
    layer = lax.axis_index("layer")
    rows, width = part.shape
    half = rows // 2
    atoms = half // BLOCK
    got = got_ref[:, got_ref.shape[1] - width:].astype(F32)
    part[...] = (piece(0, (0,), *late) + got).astype(BF16)
    flags = widen(keep_ref[...], width)

    def held(d, p):
        ref = part.at[p * half:(p + 1) * half, :] if d == 0 else moved[2 * (d - 1) + p]
        return ref[...].astype(F32)

    for value in range(4):

        @pl.when(layer == value)
        def _():
            for a in range(2):
                for p in range(2):
                    two = [held((value - 2 * a - b) % 4, p) for b in range(2)]
                    at = 2 * a + p
                    kept = tall(flags[at * atoms:(at + 1) * atoms]) > 0.5
                    out_ref[at * half:(at + 1) * half, :] = jnp.where(
                        kept, two[0] + two[1], 0.0).astype(BF16)


def total(moved, keep_t, got, acc, late):
    half, width = moved[0].shape
    return pl.pallas_call(
        total_kernel,
        out_shape=jax.ShapeDtypeStruct((4 * half, width), BF16),
        in_specs=[VM] * 14,
        out_specs=VM,
        scratch_shapes=[pltpu.VMEM((2 * half, width), BF16)],
        compiler_params=vmem(8),
        name="total",
    )(*moved, keep_t, got, acc, *late)


def stream(x, d):
    return lax.ppermute(
        x, "col", [(c, (c // 2 + (d if c % 2 == 0 else -d)) % 8 * 2 + c % 2) for c in range(16)])


def along(x, axis, d):
    return lax.ppermute(x, axis, [(i, (i + d) % 4) for i in range(4)])


def swap(x):
    return lax.ppermute(x, "col", [(c, c ^ 1) for c in range(16)])


def turn(x, d):
    pairs = []
    for r in range(4):
        for c in range(16):
            to = (r + (d if c % 2 == 0 else -d)) % 4
            pairs.append((r * 16 + c, to * 16 + c))
    return lax.ppermute(x, ("row", "col"), pairs)


def after(x, y):
    return lax.optimization_barrier((x, y))[0]


def on_device(matrix, pattern, keep):
    matrix = pltpu.with_memory_space_constraint(matrix, pltpu.HBM)
    pattern_t = pltpu.with_memory_space_constraint(pattern.T, pltpu.HBM)
    block, top, low, mine, theirs = prepare(matrix, pattern_t)
    theirs = swap(theirs)
    both = jnp.stack([mine, theirs])

    left = {0: (top, low)}
    down = block
    for step in range(1, 5):
        left[step] = tuple(stream(x, 1) for x in left[step - 1])
        if step < 4:
            down = stream(down, -1)
            left[-step] = (down, down)
    near, other = turn(both, 1), turn(both, -1)
    far = turn(after(near, (left[2], left[-2])), 1)

    steps = (0, 1, -1, 2, -2, 3)
    lefts, rights = [x for step in steps for x in left[step]], [both, near, other]
    acc = early(lefts, steps, rights)
    own, theirs, rows, meet = middle(acc, left[-3], lefts, steps, rights)
    late = [*left[4], rows, meet, far]
    sent = others((1, 3), theirs, late)
    got = swap(others((2, 0), after(theirs, sent), late))
    moved = {}
    for ds, arrived in (((1, 3), swap(sent)), ((2,), got)):
        for i, part in enumerate(owns(ds, arrived, own, late)):
            d = ds[i % len(ds)]
            moved[d, i // len(ds)] = along(part, "layer", d)
    return total([moved[d, p] for d in (1, 2, 3) for p in range(2)], keep.T, got, own, late)


def solution(mesh):
    in_specs = (P("row", "col"), P("row", "col"), P("row", ("col", "layer")))
    out_specs = P("row", ("col", "layer"))
    return jax.shard_map(
        on_device, mesh=mesh, in_specs=in_specs, out_specs=out_specs, check_vma=False
    )
```

```python
import functools

import jax
import jax.numpy as jnp
from jax import lax
from jax.experimental import pallas as pl
from jax.experimental.pallas import tpu as pltpu
from jax.sharding import PartitionSpec as P

BLOCK = 32
F32 = jnp.float32
BF16 = jnp.bfloat16
ANY = pl.BlockSpec(memory_space=pl.ANY)
HBM = pl.BlockSpec(memory_space=pltpu.HBM)
VM = pl.BlockSpec(memory_space=pltpu.VMEM)


def vmem(mib):
    return pltpu.CompilerParams(vmem_limit_bytes=mib * 1024 * 1024)


def place():
    layer = lax.axis_index("layer")
    return layer // 2, layer % 2


def widen(mask, width):
    k = mask.shape[0]
    rep = lax.broadcasted_iota(jnp.int32, (k, width), 1) // (width // k)
    one = lax.broadcasted_iota(jnp.int32, (k, width), 0)
    spread = jnp.where(rep == one, 1.0, 0.0).astype(F32)
    flag = jnp.where(mask > 0, 1.0, 0.0).astype(F32)
    return lax.dot_general(flag, spread, (((0,), (0,)), ((), ())), preferred_element_type=F32)


def tall(flags):
    n, width = flags.shape
    return jnp.broadcast_to(flags.reshape(n, 1, width), (n, BLOCK, width)).reshape(
        n * BLOCK, width
    )


def prepare_kernel(x_ref, pat_ref, block_ref, top_ref, low_ref, own_ref, send_ref, pat, wide, buf, slabs, sems):
    a, b = place()
    h = lax.axis_index("col") % 2
    rows, cols = buf.shape
    copies = [
        pltpu.make_async_copy(pat_ref, pat, sems.at[0]),
        pltpu.make_async_copy(
            x_ref.at[pl.ds(pl.multiple_of(a * rows, rows), rows),
                     pl.ds(pl.multiple_of(b * cols, cols), cols)],
            buf, sems.at[1]),
    ]
    for c in range(4):
        copies.append(pltpu.make_async_copy(
            x_ref.at[pl.ds(pl.multiple_of((2 * c + b) * cols, cols), cols), :],
            slabs.at[c], sems.at[2 + c]))
    for copy in copies:
        copy.start()
    copies[0].wait()
    wide[...] = widen(pat[...], wide.shape[1])
    copies[1].wait()
    atoms = rows // BLOCK
    flags = wide[pl.ds(pl.multiple_of(a * atoms, atoms), atoms),
                 pl.ds(pl.multiple_of(b * cols, cols), cols)]
    half = rows // 2
    for part, ref in enumerate((top_ref, low_ref)):
        at = slice(part * half, (part + 1) * half)
        kept = buf[at, :] * tall(flags[part * atoms // 2:(part + 1) * atoms // 2]).astype(BF16)
        ref[...] = kept
        block_ref[at, :] = kept
    atoms = cols // BLOCK
    for copy in copies[2:]:
        copy.wait()
    for i in range(2):
        for ref, k in ((own_ref, 2 * i + h), (send_ref, 2 * i + 1 - h)):
            at = pl.ds(pl.multiple_of((2 * k + b) * atoms, atoms), atoms)
            ref[i * cols:(i + 1) * cols, :] = slabs[k] * tall(wide[at, :]).astype(BF16)


def prepare(matrix, pattern_t):
    rows, cols = matrix.shape
    block = jax.ShapeDtypeStruct((rows // 2, cols // 2), BF16)
    left = jax.ShapeDtypeStruct((rows // 4, cols // 2), BF16)
    right = jax.ShapeDtypeStruct((cols, cols), BF16)
    return pl.pallas_call(
        prepare_kernel,
        out_shape=(block, left, left, right, right),
        in_specs=[HBM, HBM],
        out_specs=(VM,) * 5,
        scratch_shapes=[
            pltpu.VMEM(pattern_t.shape, jnp.int32),
            pltpu.VMEM((rows // BLOCK, cols), F32),
            pltpu.VMEM((rows // 2, cols // 2), BF16),
            pltpu.VMEM((4, cols // 2, cols), BF16),
            pltpu.SemaphoreType.DMA((6,)),
        ],
        compiler_params=vmem(12),
        name="prepare",
    )(matrix, pattern_t)


def side():
    return 1 - 2 * (lax.axis_index("col") % 2)


def meeting(step):
    source = lax.rem(lax.axis_index("col") // 2 - step * side() + 8, 8)
    away = lax.rem((lax.axis_index("row") - source // 2) * side() + 8, 4)
    return away, lax.rem(source, 2)


def halves(refs):
    return [refs[i:i + 2] for i in range(0, len(refs), 2)]


def rows_of(ref, half, part):
    return ref if ref.shape[0] == half else ref.at[pl.ds(part * half, half), :]


def early_kernel(steps, *refs):
    n = len(steps)
    lefts, refs = halves(refs[:2 * n]), refs[2 * n:]
    (own, near, other), outs, (left, right, lsem, rsem) = refs[:3], refs[3:5], refs[5:]
    rows, cols = outs[0].shape
    half, width = lefts[0][0].shape
    waits = []
    for i, step in enumerate(steps):
        away, low = meeting(step)
        low = pl.multiple_of(low * width, width)
        for part in range(2):
            copy = pltpu.make_async_copy(
                rows_of(lefts[i][part], half, part),
                left.at[pl.ds(part * half, half), pl.ds(i * width, width)], lsem.at[i, part])
            waits.append((copy, away != 2))
            pl.when(away != 2)(copy.start)

        @pl.when(away == 2)
        def _():
            left[:, i * width:(i + 1) * width] = jnp.zeros((rows, width), BF16)

        for ref, here in ((own, (away == 0) | (away == 2)), (near, away == 1), (other, away == 3)):
            for slot in range(2):
                copy = pltpu.make_async_copy(
                    ref.at[slot, pl.ds(low, width), :],
                    right.at[pl.ds(i * width, width), pl.ds(slot * cols, cols)],
                    rsem.at[i, slot])
                waits.append((copy, here))
                pl.when(here)(copy.start)
    for copy, here in waits:
        pl.when(here)(copy.wait)
    for slot in range(2):
        outs[slot][...] = jnp.dot(
            left[...], right[:, slot * cols:(slot + 1) * cols], preferred_element_type=F32)


def early(lefts, steps, rights):
    rows, width = 2 * lefts[0].shape[0], lefts[0].shape[1]
    cols = rights[0].shape[2]
    n = len(steps)
    out = jax.ShapeDtypeStruct((rows, cols), F32)
    return pl.pallas_call(
        functools.partial(early_kernel, steps),
        out_shape=(out,) * 2,
        in_specs=[ANY] * (2 * n + 3),
        out_specs=(VM,) * 2,
        scratch_shapes=[
            pltpu.VMEM((rows, n * width), BF16),
            pltpu.VMEM((n * width, 2 * cols), BF16),
            pltpu.SemaphoreType.DMA((n, 2)),
            pltpu.SemaphoreType.DMA((n, 2)),
        ],
        compiler_params=vmem(16),
        name="early",
    )(*lefts, *rights)


def middle_kernel(steps, *refs):
    n = len(steps)
    own_ref, other_ref, *end = refs[:4]
    lefts, refs = halves(refs[4:4 + 2 * n]), refs[4 + 2 * n:]
    rights, refs = refs[:3], refs[3:]
    own_out, other_out, rows_out, left_out, right, lsem, rsem = refs
    rows, width = end[0].shape
    half = rows // 2
    cols = own_out.shape[1]
    z, r = lax.axis_index("col") // 2, lax.axis_index("row")
    waits = []

    def copy(source, target, sem, here):
        one = pltpu.make_async_copy(source, target, sem)
        pl.when(here)(one.start)
        waits.append(lambda: pl.when(here)(one.wait))

    for i, (step, ref) in enumerate(((-3, right), (4, rows_out))):
        away, low = meeting(step)
        low = pl.multiple_of(low * width, width)
        for j, source in zip((0, 1, 3), rights):
            for slot in range(2):
                copy(source.at[slot, pl.ds(low, width), :],
                     ref.at[:, pl.ds(slot * cols, cols)], rsem.at[i, slot], away == j)

        @pl.when(away == 2)
        def _():
            ref[...] = jnp.zeros_like(ref)

    for q in range(2):
        source = 2 * lax.rem(r + 2, 4) + q
        step = lax.rem((z - source) * side() + 16, 8)
        at = pl.ds(q * width, width)
        for i, ref in enumerate([*lefts, end]):
            for part in range(2):
                copy(rows_of(ref[part], half, part), left_out.at[pl.ds(part * half, half), at], lsem.at[q, part],
                     step == (*steps, -3)[i] % 8)

        @pl.when(step == 4)
        def _():
            left_out[:, q * width:(q + 1) * width] = jnp.zeros((rows, width), BF16)

    for wait in waits:
        wait()
    for slot, (ref, out) in enumerate(((own_ref, own_out), (other_ref, other_out))):
        for part in range(2):
            at = slice(part * half, (part + 1) * half)
            out[at, :] = ref[at, :] + jnp.dot(
                end[part][at, :], right[:, slot * cols:(slot + 1) * cols],
                preferred_element_type=F32)


def middle(acc, end, lefts, steps, rights):
    rows, width = end[0].shape
    cols = acc[0].shape[1]
    n = len(steps)
    out = jax.ShapeDtypeStruct((rows, cols), F32)
    return pl.pallas_call(
        functools.partial(middle_kernel, steps),
        out_shape=(
            out, out,
            jax.ShapeDtypeStruct((width, 2 * cols), BF16),
            jax.ShapeDtypeStruct((rows, 2 * width), BF16),
        ),
        in_specs=[VM] * 4 + [ANY] * (2 * n + 3),
        out_specs=(VM,) * 4,
        scratch_shapes=[
            pltpu.VMEM((width, 2 * cols), BF16),
            pltpu.SemaphoreType.DMA((2, 2)),
            pltpu.SemaphoreType.DMA((2, 2)),
        ],
        compiler_params=vmem(16),
        name="middle",
    )(*acc, *end, *lefts, *rights)


def columns(ref, ds, base, width):
    layer = lax.axis_index("layer")
    parts = [
        ref[:, pl.ds(pl.multiple_of(base + lax.rem(layer + d, 4) * width, width), width)]
        for d in ds
    ]
    return parts[0] if len(parts) == 1 else jnp.concatenate(parts, axis=1)


def piece(slot, ds, acc_ref, top_ref, low_ref, rows_ref, left_ref, far_ref):
    cols = acc_ref.shape[1]
    width = cols // 4
    away, low = meeting(4)
    deep = rows_ref.shape[0]
    here = pl.ds(pl.multiple_of(low * deep, deep), deep)
    rows = jnp.where(
        away == 2,
        columns(far_ref.at[slot, here, :], ds, 0, width),
        columns(rows_ref, ds, slot * cols, width))
    last = [jnp.dot(ref[...], rows, preferred_element_type=F32) for ref in (top_ref, low_ref)]
    return (
        columns(acc_ref, ds, 0, width)
        + jnp.concatenate(last, axis=0)
        + jnp.dot(left_ref[...], columns(far_ref.at[slot], ds, 0, width), preferred_element_type=F32)
    )


def others_kernel(ds, *refs):
    refs[-1][...] = piece(1, ds, *refs[:-1]).astype(BF16)


def others(ds, acc, late):
    rows, cols = acc.shape
    return pl.pallas_call(
        functools.partial(others_kernel, ds),
        out_shape=jax.ShapeDtypeStruct((rows, cols // 4 * len(ds)), BF16),
        in_specs=[VM] * 6,
        out_specs=VM,
        compiler_params=vmem(6),
        name="others",
    )(acc, *late)


def owns_kernel(ds, skip, *refs):
    (got_ref, *refs), outs = refs[:7], refs[7:]
    width = outs[0].shape[1]
    sums = piece(0, ds, *refs) + got_ref[:, skip * width:(skip + len(ds)) * width].astype(F32)
    half = outs[0].shape[0]
    for i, out in enumerate(outs):
        k, part = i % len(ds), i // len(ds)
        out[...] = sums[part * half:(part + 1) * half, k * width:(k + 1) * width].astype(BF16)


def owns(ds, got, acc, late, skip=0):
    rows, cols = acc.shape
    return pl.pallas_call(
        functools.partial(owns_kernel, ds, skip),
        out_shape=(jax.ShapeDtypeStruct((rows // 2, cols // 4), BF16),) * (2 * len(ds)),
        in_specs=[VM] * 7,
        out_specs=(VM,) * (2 * len(ds)),
        compiler_params=vmem(4),
        name="owns",
    )(got, acc, *late)


def total_kernel(*refs):
    pieces, (keep_ref, out_ref) = refs[:8], refs[8:]
    layer = lax.axis_index("layer")
    half, width = pieces[0].shape
    atoms = half // BLOCK
    flags = widen(keep_ref[...], width)

    def held(d, p):
        return pieces[2 * d + p][...].astype(F32)

    for value in range(4):

        @pl.when(layer == value)
        def _():
            for a in range(2):
                for p in range(2):
                    two = [held((value - 2 * a - b) % 4, p) for b in range(2)]
                    at = 2 * a + p
                    kept = tall(flags[at * atoms:(at + 1) * atoms]) > 0.5
                    out_ref[at * half:(at + 1) * half, :] = jnp.where(
                        kept, two[0] + two[1], 0.0).astype(BF16)


def total(pieces, keep_t):
    half, width = pieces[0].shape
    return pl.pallas_call(
        total_kernel,
        out_shape=jax.ShapeDtypeStruct((4 * half, width), BF16),
        in_specs=[VM] * 9,
        out_specs=VM,
        compiler_params=vmem(8),
        name="total",
    )(*pieces, keep_t)


def stream(x, d):
    return lax.ppermute(
        x, "col", [(c, (c // 2 + (d if c % 2 == 0 else -d)) % 8 * 2 + c % 2) for c in range(16)])


def along(x, axis, d):
    return lax.ppermute(x, axis, [(i, (i + d) % 4) for i in range(4)])


def swap(x):
    return lax.ppermute(x, "col", [(c, c ^ 1) for c in range(16)])


def turn(x, d):
    pairs = []
    for r in range(4):
        for c in range(16):
            to = (r + (d if c % 2 == 0 else -d)) % 4
            pairs.append((r * 16 + c, to * 16 + c))
    return lax.ppermute(x, ("row", "col"), pairs)


def after(x, y):
    return lax.optimization_barrier((x, y))[0]


def on_device(matrix, pattern, keep):
    matrix = pltpu.with_memory_space_constraint(matrix, pltpu.HBM)
    pattern_t = pltpu.with_memory_space_constraint(pattern.T, pltpu.HBM)
    block, top, low, mine, theirs = prepare(matrix, pattern_t)
    theirs = swap(theirs)
    both = jnp.stack([mine, theirs])

    left = {0: (top, low)}
    down = block
    for step in range(1, 5):
        left[step] = tuple(stream(x, 1) for x in left[step - 1])
        if step < 4:
            down = stream(down, -1)
            left[-step] = (down, down)
    near, other = turn(both, 1), turn(both, -1)
    far = turn(after(near, (left[2], left[-2])), 1)

    steps = (0, 1, -1, 2, -2, 3)
    lefts, rights = [x for step in steps for x in left[step]], [both, near, other]
    acc = early(lefts, steps, rights)
    own, theirs, rows, meet = middle(acc, left[-3], lefts, steps, rights)
    late = [*left[4], rows, meet, far]
    sent = others((1, 3), theirs, late)
    got = swap(others((2, 0), after(theirs, sent), late))
    moved = {}
    for ds, arrived in (((1, 3), swap(sent)), ((2,), got)):
        for i, part in enumerate(owns(ds, arrived, own, late)):
            d = ds[i % len(ds)]
            moved[d, i // len(ds)] = along(part, "layer", d)
    moved[0, 0], moved[0, 1] = owns((0,), got, own, late, 1)
    return total([moved[d, p] for d in range(4) for p in range(2)], keep.T)


def solution(mesh):
    in_specs = (P("row", "col"), P("row", "col"), P("row", ("col", "layer")))
    out_specs = P("row", ("col", "layer"))
    return jax.shard_map(
        on_device, mesh=mesh, in_specs=in_specs, out_specs=out_specs, check_vma=False
    )
```
